256 devices in a mesh: bricks: 64 (over y, z, core), slab: 4 (over x).
Axes of the slice: x: 4, y: 4, z: 8, core: 2. Of those that a mesh axis runs over, the one named last changes fastest.
Arguments:
- part_pos: float32 [256, 3, 2048], P(('bricks', 'slab')), may hold values from 0 to 1, as said below
- part_mass: float32 [256, 2048], P(('bricks', 'slab')), may hold values from 0.5 to 2
- cell_pos: float32 [256, 3, 2048], P(('bricks', 'slab')), may hold values from 0 to 1, as said below
- cell_mass: float32 [256, 2048], P(('bricks', 'slab')), may hold values from 0.5 to 2
- cell_scale: float32 [256, 2048], P(('bricks', 'slab')), may hold values from 0.5 to 2
- req_tile: int32 [16384, 1], P(('bricks', 'slab')), may hold values from 0 to 15, as said below
- tile_bucket: int32 [256, 144], P(('bricks', 'slab')), may hold values from 0 to 15, as said below
- tile_slot: int32 [256, 144], P(('bricks', 'slab')), may hold values from 0 to 63, as said below
- tile_count: int32 [256], P(('bricks', 'slab')), may hold values from 64 to 144, as said below
- lagr_index: int32 [256, 2048], P(('bricks', 'slab')), may hold values from 0 to 2047, each once within a row
Outputs:
- particle_potential: float32 [256, 2048], P(('bricks', 'slab'))
- cell_potential: float32 [256, 2048], P(('bricks', 'slab'))
- divergence: float32 [16, 256, 128], P('slab', 'bricks')
The draws below stay inside these ranges and needn't reach their ends.
Inputs may be any that keep to these rules, and one draw needn't show every extreme that they name: `part_pos`: device b * 4 + s holds particles of its own brick: component 0 within [0.25 b / 64, 0.25 (b + 1) / 64], component 1 within [0.25 s / 4, 0.25 (s + 1) / 4], component 2 within [0, 1]. `cell_pos`: device b * 4 + s holds the cells of the same brick, bounded as its particles. `req_tile`: over the devices of one slab index, every cell tile of every device is named by exactly four slots. `tile_bucket`: A device's live tiles name each of its buckets at least once. `tile_slot`: A device's live tiles name each of its slots at least once. `tile_count`: the live tiles are the first entries of a device's list; one device has exactly 144, every other between 64 and 80. `lagr_index`: each device's particles fill its block of the Lagrangian grid, one point each.
All inputs are finite; a program needn't handle non-finite values.
Results may differ from the reference program's by a relative error of at most 0.0003.
Values sent between devices are 32-bit elements; how exact they have to be, the bound alone decides.
A program may use at most 64 MiB of HBM per device.

```python
import math
import jax
import jax.numpy as jnp
from jax import lax

TS = 128
ITERS = 2
LB = 4
BK_DEV = 16
CT_DEV = 16
SLOTS = 64
CAP = 1
TILE_DEV = 144
PART_DEV = 2048
CELL_DEV = 2048
LA = 4
NA = 16
NL = 256
N_BRICKS = 64
N_SLAB = 4
DEVICES = 256


def brick_points(key, count):
    unit = jax.random.uniform(key, (DEVICES, 3, count), jnp.float32, 0.0, 1.0)
    device_ids = jnp.arange(DEVICES, dtype=jnp.int32)
    brick_ids = (device_ids // N_SLAB).astype(jnp.float32)
    slab_ids = (device_ids % N_SLAB).astype(jnp.float32)
    first = 0.25 * (brick_ids[:, None] + unit[:, 0, :]) / N_BRICKS
    second = 0.25 * (slab_ids[:, None] + unit[:, 1, :]) / N_SLAB
    return jnp.stack([first, second, unit[:, 2, :]], axis=1).astype(jnp.float32)


def draw_part_pos(key, part):
    return brick_points(jax.random.fold_in(key, 31), PART_DEV)


def draw_cell_pos(key, part):
    return brick_points(jax.random.fold_in(key, 32), CELL_DEV)


def tile_lists(key):

    def one_device(device_key):
        keys = jax.random.split(device_key, 5)
        slot_cover = jax.random.permutation(keys[0], SLOTS).astype(jnp.int32)
        slot_extra = jax.random.randint(keys[1], (TILE_DEV - SLOTS,), 0, SLOTS).astype(jnp.int32)
        bucket_cover = jax.random.permutation(keys[2], BK_DEV).astype(jnp.int32)
        bucket_extra = jax.random.randint(keys[3], (TILE_DEV - BK_DEV,), 0, BK_DEV).astype(jnp.int32)
        head_order = jax.random.permutation(keys[4], SLOTS).astype(jnp.int32)
        order = jnp.concatenate([head_order, jnp.arange(SLOTS, TILE_DEV, dtype=jnp.int32)])
        slot_list = jnp.concatenate([slot_cover, slot_extra])[order]
        bucket_list = jnp.concatenate([bucket_cover, bucket_extra])[order]
        return (slot_list.astype(jnp.int32), bucket_list.astype(jnp.int32))
    device_keys = jax.random.split(jax.random.fold_in(key, 11), DEVICES)
    slot_lists, bucket_lists = jax.vmap(one_device)(device_keys)
    counts = jax.random.randint(jax.random.fold_in(key, 12), (DEVICES,), SLOTS, SLOTS + SLOTS // 4 + 1)
    busiest = jax.random.randint(jax.random.fold_in(key, 13), (), 0, DEVICES)
    counts = jnp.where(jnp.arange(DEVICES) == busiest, TILE_DEV, counts)
    return (slot_lists, bucket_lists, counts.astype(jnp.int32))


def draw_tile_slot(key, part):
    return tile_lists(key)[0]


def draw_tile_bucket(key, part):
    return tile_lists(key)[1]


def draw_tile_count(key, part):
    return tile_lists(key)[2]


def owner_table(owner_key):
    return jax.random.permutation(owner_key, SLOTS).astype(jnp.int32) % CT_DEV


def draw_req_tile(key, part):
    owner_keys = jax.random.split(jax.random.fold_in(key, 21), DEVICES)
    table = jax.vmap(owner_table)(owner_keys)
    table = table.reshape(N_BRICKS, N_SLAB, N_BRICKS, CAP).transpose(2, 1, 0, 3)
    return table.reshape(DEVICES * N_BRICKS, CAP).astype(jnp.int32)


def levels(own_key, dims, pieces, smallest, largest):
    gain = 1.0
    for position, parts in pieces:
        draws = jax.random.uniform(jax.random.fold_in(jax.random.fold_in(own_key, 6), position), (parts,), jnp.float32, smallest / len(pieces), largest / len(pieces))
        gain = gain * jnp.repeat(jnp.exp(draws), dims[position] // parts).reshape((-1,) + (1,) * (len(dims) - 1 - position))
    return gain


def setup_inputs(seed: int = 0) -> dict:
    key_list = jax.random.split(jax.random.key(seed), 11)
    return {
        "part_pos": draw_part_pos(jax.random.fold_in(key_list[10], 71), 0),
        "part_mass": jnp.clip(jnp.exp(math.log(2.0) - 1.3862944 * jax.random.uniform(key_list[1], (DEVICES, PART_DEV), jnp.float32) ** levels(key_list[1], (DEVICES, PART_DEV), ((0, 256),), -0.2, 0.2)), 0.5, 2.0),
        "cell_pos": draw_cell_pos(jax.random.fold_in(key_list[10], 71), 0),
        "cell_mass": jnp.clip(jnp.exp(math.log(2.0) - 1.3862944 * jax.random.uniform(key_list[3], (DEVICES, CELL_DEV), jnp.float32) ** levels(key_list[3], (DEVICES, CELL_DEV), ((0, 256),), -0.2, 0.2)), 0.5, 2.0),
        "cell_scale": jnp.clip(jnp.exp(math.log(2.0) - 1.3862944 * jax.random.uniform(key_list[4], (DEVICES, CELL_DEV), jnp.float32) ** levels(key_list[4], (DEVICES, CELL_DEV), ((0, 256),), -0.2, 0.2)), 0.5, 2.0),
        "req_tile": draw_req_tile(jax.random.fold_in(key_list[10], 71), 0),
        "tile_bucket": draw_tile_bucket(jax.random.fold_in(key_list[10], 71), 0),
        "tile_slot": draw_tile_slot(jax.random.fold_in(key_list[10], 71), 0),
        "tile_count": draw_tile_count(jax.random.fold_in(key_list[10], 71), 0),
        "lagr_index": jax.vmap(lambda own: jax.random.permutation(own, PART_DEV))(jax.random.split(key_list[9], DEVICES)).reshape((DEVICES, PART_DEV)).astype(jnp.int32),
    }


EPS = 0.05


def tile_kernel(part_tiles, cell_tiles, live_mask):
    distance = (part_tiles[:, 0, :, None] - cell_tiles[:, 0, None, :]) ** 2
    distance = distance + (part_tiles[:, 1, :, None] - cell_tiles[:, 1, None, :]) ** 2
    distance = distance + (part_tiles[:, 2, :, None] - cell_tiles[:, 2, None, :]) ** 2
    return jnp.exp(-distance / EPS) * live_mask[:, None, None]


def place_values(values, order):
    return jnp.zeros_like(values).at[:, order].set(values)


def reference(part_pos, part_mass, cell_pos, cell_mass, cell_scale, req_tile, tile_bucket, tile_slot, tile_count, lagr_index):
    device_count = N_BRICKS * N_SLAB
    dev_ids = jnp.arange(device_count, dtype=jnp.int32)
    owners = jnp.arange(N_BRICKS, dtype=jnp.int32)[None, :] * N_SLAB + (dev_ids % N_SLAB)[:, None]
    owner_rows = jnp.repeat(owners, CAP, axis=1)
    wanted = req_tile.reshape(device_count, SLOTS)
    own_cells = cell_pos.reshape(device_count, 3, CT_DEV, TS).transpose(0, 2, 1, 3)
    slot_cells = own_cells[owner_rows, wanted]
    part_tiles = part_pos.reshape(device_count, 3, BK_DEV, TS).transpose(0, 2, 1, 3)
    live_mask = (jnp.arange(TILE_DEV, dtype=jnp.int32)[None, :] < tile_count[:, None]).astype(jnp.float32)
    bucket_ids = jnp.arange(BK_DEV, dtype=jnp.int32)
    slot_ids = jnp.arange(SLOTS, dtype=jnp.int32)

    def kernels(index):
        return tile_kernel(part_tiles[index][tile_bucket[index]], slot_cells[index][tile_slot[index]], live_mask[index])

    def row_sums(values):
        slot_values = values[owner_rows, wanted]

        def one_device(index):
            kernel = kernels(index)
            per_tile = jnp.einsum("tij,tcj->tci", kernel, slot_values[index][tile_slot[index]], precision=lax.Precision.HIGHEST)
            one_hot = (tile_bucket[index][:, None] == bucket_ids[None, :]).astype(jnp.float32)
            return jnp.einsum("tb,tci->bci", one_hot, per_tile, precision=lax.Precision.HIGHEST)

        return lax.map(one_device, dev_ids)

    def column_sums(particle_scale):
        def one_device(index):
            kernel = kernels(index)
            per_tile = jnp.einsum("tij,ti->tj", kernel, particle_scale[index][tile_bucket[index]], precision=lax.Precision.HIGHEST)
            one_hot = (tile_slot[index][:, None] == slot_ids[None, :]).astype(jnp.float32)
            return jnp.einsum("ts,tj->sj", one_hot, per_tile, precision=lax.Precision.HIGHEST)

        partial_value = lax.map(one_device, dev_ids)
        return jnp.zeros((device_count, CT_DEV, TS), jnp.float32).at[owner_rows, wanted].add(partial_value)

    masses = part_mass.reshape(device_count, BK_DEV, TS)
    cell_masses = cell_mass.reshape(device_count, CT_DEV, TS)
    cell_scaling = cell_scale.reshape(device_count, CT_DEV, TS)
    for sweep in range(ITERS):
        totals = row_sums(cell_scaling[:, :, None, :])
        particle_scale = masses / totals[:, :, 0]
        cell_scaling = cell_masses / column_sums(particle_scale)
    weighted = jnp.concatenate([cell_scaling[:, :, None, :], cell_scaling[:, :, None, :] * own_cells], axis=2)
    totals = row_sums(weighted)
    particle_scale = masses / totals[:, :, 0]
    displacement = totals[:, :, 1:] / totals[:, :, 0:1] - part_tiles
    displacement = displacement.transpose(0, 2, 1, 3).reshape(device_count, 3, PART_DEV)
    placed = jax.vmap(place_values)(displacement, lagr_index)
    lagr_field = placed.reshape(N_BRICKS, N_SLAB, 3, LA, LB, TS).transpose(2, 1, 3, 0, 4, 5).reshape(3, NA, NL, TS)
    padded = jnp.pad(lagr_field, ((0, 0), (1, 1), (1, 1), (1, 1)))
    divergence = 0.5 * (padded[0, 2:, 1:-1, 1:-1] - padded[0, :-2, 1:-1, 1:-1])
    divergence = divergence + 0.5 * (padded[1, 1:-1, 2:, 1:-1] - padded[1, 1:-1, :-2, 1:-1])
    divergence = divergence + 0.5 * (padded[2, 1:-1, 1:-1, 2:] - padded[2, 1:-1, 1:-1, :-2])
    particle_potential = jnp.log(particle_scale).reshape(device_count, PART_DEV)
    cell_potential = jnp.log(cell_scaling).reshape(device_count, CELL_DEV)
    return (particle_potential, cell_potential, divergence)
```

```python
import functools
import math

import jax
import jax.numpy as jnp
from jax import lax
from jax.experimental import pallas as pl
from jax.experimental.pallas import tpu as pltpu
from jax.sharding import PartitionSpec as P

TS = 128
EPS = 0.05
ITERS = 2
LB = 4
SCALE = math.sqrt(2.0 / (EPS * math.log(2.0)))
CENTER = (0.125, 0.125, 0.5)
HALF_LN2 = 0.5 * math.log(2.0)
MESH = pl.DeviceIdType.MESH
F32, BF16, I32 = jnp.float32, jnp.bfloat16, jnp.int32
TL = 256


def split3(a):
    hi = a.astype(BF16)
    rest = a - hi.astype(F32)
    mid = rest.astype(BF16)
    return hi, mid, (rest - mid.astype(F32)).astype(BF16)


def pick(hot, rows):
    hi, mid, lo = split3(rows)
    return jnp.dot(
        jnp.concatenate([hot, hot, hot], axis=1),
        jnp.concatenate([hi, mid, lo], axis=0),
        preferred_element_type=F32,
    )


def iota(shape, axis):
    return lax.broadcasted_iota(I32, shape, axis)


def kernel(
    nb, ns, buckets, tiles, count,
    pos_in, mass_in, cpos_in, cmass_in, cscale_in, req_in, tb_in, ts_in, cnt_in, lagr_in,
    pp_out, cp_out, div_out,
    ask, asked, lists_v, lists, xs, ys, rowsets, xb, mb, ub, kt, seg, colseg,
    pay, cells, wsend, wrecv, vsend, vrecv, vy, hot_l, field, halo,
    ssem, rsem, hsem, lsem,
):
    me, sl = lax.axis_index("bricks"), lax.axis_index("slab")
    up, down = lax.rem(me + 1, nb), lax.rem(me + nb - 1, nb)
    right, left = lax.rem(sl + 1, ns), lax.rem(sl + ns - 1, ns)

    barrier = pltpu.get_barrier_semaphore()

    def greet(k, carry):
        pl.semaphore_signal(
            barrier, inc=1, device_id=(lax.rem(me + k, nb), sl), device_id_type=MESH
        )
        return carry

    lax.fori_loop(1, nb, greet, 0)
    for other in (left, right):
        pl.semaphore_signal(barrier, inc=1, device_id=(me, other), device_id_type=MESH)

    def send_all(src, dst, phase):
        def one(k, carry):
            peer = lax.rem(me + k, nb)
            pltpu.make_async_remote_copy(
                src_ref=src.at[peer], dst_ref=dst.at[me],
                send_sem=ssem.at[phase], recv_sem=rsem.at[phase],
                device_id=(peer, sl), device_id_type=MESH,
            ).start()
            return carry

        lax.fori_loop(1, nb, one, 0)
        pltpu.make_async_copy(src.at[me], dst.at[me], rsem.at[phase]).start()

    def wait_all(dst, phase):
        pltpu.make_async_copy(dst, dst, rsem.at[phase]).wait()

    def wait_sent(src, phase):
        part = src.at[pl.ds(0, nb - 1)]
        pltpu.make_async_copy(part, part, ssem.at[phase]).wait()

    ask[...] = jnp.broadcast_to(req_in[...], ask.shape)

    pl.semaphore_wait(barrier, nb + 1)
    send_all(ask, asked, 0)

    lane = iota((1, TL), 1)
    live = lane < cnt_in[0]
    tb = jnp.concatenate([tb_in[...], jnp.zeros((1, TL - count), I32)], axis=1)
    ts = jnp.concatenate([ts_in[...], jnp.zeros((1, TL - count), I32)], axis=1)
    key_b = jnp.where(live, tb, buckets)
    key_s = jnp.where(live, ts, nb)
    uni_b, uni_s = key_b * TL + lane, key_s * TL + lane
    zero = jnp.zeros((1, TL), I32)
    cols = jnp.concatenate([uni_b, uni_s, tb, ts, key_b, key_s, zero, zero], axis=0).T
    col_tb, col_ts, col_kb, col_ks = (cols[:, i : i + 1] for i in range(2, 6))

    def total(where, value):
        return jnp.sum(jnp.where(where, value, 0), axis=0, keepdims=True)

    rank_b = total(cols[:, 0:1] < uni_b, 1)
    rank_s = total(cols[:, 1:2] < uni_s, 1)
    ranks = jnp.concatenate([rank_b, rank_s] + [zero] * 6, axis=0).T
    wide = iota((TL, TL), 1)
    at_b, at_s = ranks[:, 0:1] == wide, ranks[:, 1:2] == wide

    def same(row):
        return jnp.where((row == pltpu.roll(row, 1, 1)) & (lane > 0), 1, 0)

    def within(row, most):
        return jnp.minimum(jnp.maximum(row, 0), most)

    lists_v[0:1, :] = within(total(at_b, col_tb), buckets - 1)
    lists_v[1:2, :] = within(total(at_b, col_ts), nb - 1)
    lists_v[2:3, :] = same(total(at_b, col_kb))
    lists_v[3:4, :] = within(total(at_s, ranks[:, 0:1]), count - 1)
    lists_v[4:5, :] = within(total(at_s, col_tb), buckets - 1)
    lists_v[5:6, :] = same(total(at_s, col_ks))
    lists_v[6:7, :] = within(total(col_kb <= wide, 1) - 1, count - 1)
    lists_v[7:8, :] = within(total(col_ks <= wide, 1) - 1, count - 1)
    to_smem = pltpu.make_async_copy(lists_v, lists, lsem)
    to_smem.start()

    for q in range(buckets):
        part = pl.ds(q * TS, TS)
        rowsets[0, q : q + 1, :] = mass_in[:, part]
        for m in range(3):
            xs[m, q : q + 1, :] = (pos_in[0, m : m + 1, part] - CENTER[m]) * SCALE
    for q in range(tiles):
        part = pl.ds(q * TS, TS)
        rowsets[1, q : q + 1, :] = cmass_in[:, part]
        rowsets[2, q : q + 1, :] = cscale_in[:, part]
        for m in range(3):
            ys[m, q : q + 1, :] = (cpos_in[0, m : m + 1, part] - CENTER[m]) * SCALE
    ysq = ys[0] * ys[0] + ys[1] * ys[1] + ys[2] * ys[2]
    scaled = rowsets[2] * jnp.exp2(-0.5 * ysq)
    offer = jnp.concatenate([ys[0], ys[1], ys[2], scaled, rowsets[1]], axis=1)

    columns = jnp.concatenate([xs[0], xs[1], xs[2], rowsets[0]], axis=0).T
    for q in range(buckets):
        for m in range(3):
            xb[m, q] = jnp.broadcast_to(columns[:, m * buckets + q : m * buckets + q + 1], (TS, TS))
        mb[q] = jnp.broadcast_to(columns[:, 3 * buckets + q : 3 * buckets + q + 1], (TS, TS))

    wait_all(asked, 0)
    asks = asked[...].astype(F32)
    hot = jnp.where(asks[:, 0:tiles] == iota((nb, tiles), 1).astype(F32), 1.0, 0.0).astype(BF16)
    chosen = pick(hot, offer)
    for m in range(4):
        pay[:, m, :] = chosen[:, m * TS : (m + 1) * TS]
    send_all(pay, cells, 1)
    cmass_of = chosen[:, 4 * TS :]
    asks_t = asks.T
    twins = jnp.where(asks[:, 0:nb] == asks_t[0:nb, :], 1.0, 0.0).astype(BF16)
    hot_t = jnp.where(asks_t[0:tiles, :] == iota((tiles, nb), 0).astype(F32), 1.0, 0.0).astype(BF16)

    for q in range(buckets):
        vy[0, q : q + 1, :] = lagr_in[:, pl.ds(q * TS, TS)].astype(F32)
    spots = vy[0, 0:buckets, :]
    spots_c = jnp.concatenate([spots, jnp.zeros((TS - buckets, TS), F32)], axis=0).T
    for q in range(buckets):
        spot = jnp.broadcast_to(spots_c[:, q : q + 1], (TS, TS)).astype(I32)
        hot_l[q] = jnp.where(lax.rem(spot, TS) == iota((TS, TS), 1), 1.0, 0.0).astype(BF16)

    to_smem.wait()
    wait_all(cells, 1)

    def build(k, total):
        b, s = lists[0, k], lists[1, k]
        exponent = xb[0, b] * cells[s, 0:1] + xb[1, b] * cells[s, 1:2] + xb[2, b] * cells[s, 2:3]
        tile = jnp.exp2(exponent)
        kt[k] = tile
        total = jnp.where(lists[2, k] > 0, total, 0.0) + tile * cells[s, 3:4]
        seg[k] = total
        return total

    lax.fori_loop(0, count, build, jnp.zeros((TS, TS), F32), unroll=4)

    def row_pass(value):
        def step(k, total):
            total = jnp.where(lists[2, k] > 0, total, 0.0) + kt[k] * value(lists[1, k])
            seg[k] = total
            return total

        lax.fori_loop(0, count, step, jnp.zeros((TS, TS), F32), unroll=4)

    def col_pass(phase):
        def scale(q, carry):
            ub[q] = mb[q] / jnp.sum(seg[lists[6, q]], axis=1, keepdims=True)
            return carry

        lax.fori_loop(0, buckets, scale, 0, unroll=2)

        def step(k, total):
            product = kt[lists[3, k]] * ub[lists[4, k]]
            part = jnp.sum(product.reshape(TS // 8, 8, TS), axis=0)
            total = jnp.where(lists[5, k] > 0, total, 0.0) + part
            colseg[k] = total
            return total

        lax.fori_loop(0, count, step, jnp.zeros((8, TS), F32), unroll=8)

        def gather(s, carry):
            wsend[phase, pl.ds(s, 1), :] = jnp.sum(colseg[lists[7, s]], axis=0, keepdims=True)
            return carry

        lax.fori_loop(0, nb, gather, 0, unroll=8)

    for sweep in range(ITERS):
        if sweep:
            row_pass(lambda s: vrecv[0, pl.ds(s, 1), :])
        col_pass(sweep)
        send_all(wsend.at[sweep], wrecv.at[sweep], 2 + 2 * sweep)
        wait_all(wrecv.at[sweep], 2 + 2 * sweep)
        vsend[sweep] = cmass_of / pick(twins, wrecv[sweep])
        send_all(vsend.at[sweep], vrecv.at[sweep], 3 + 2 * sweep)
        if sweep == ITERS - 1:
            cell_v = rowsets[1] / pick(hot_t, wrecv[sweep])
            potential = jnp.log(cell_v) + HALF_LN2 * ysq
            for q in range(tiles):
                cp_out[:, pl.ds(q * TS, TS)] = potential[q : q + 1, :]
        wait_all(vrecv.at[sweep], 3 + 2 * sweep)

    last = vrecv[ITERS - 1]
    for m in range(3):
        vy[m] = last * cells[:, m, :]
    sums = jnp.zeros((TS, TS), F32)
    for m in range(4):
        if m == 3:
            row_pass(lambda s: vrecv[ITERS - 1, pl.ds(s, 1), :])
        else:
            row_pass(lambda s, m=m: vy[m, pl.ds(s, 1), :])

        def place(q, carry, m=m):
            total = jnp.sum(seg[lists[6, q]], axis=1, keepdims=True)
            return jnp.where(iota((TS, TS), 1) == q + m * buckets, total, carry)

        sums = lax.fori_loop(0, buckets, place, sums, unroll=2)
    sums = sums.T
    s0 = sums[3 * buckets : 4 * buckets, :]
    masses = rowsets[0]
    xsq = xs[0] * xs[0] + xs[1] * xs[1] + xs[2] * xs[2]
    potential = jnp.log(masses / s0) + HALF_LN2 * xsq
    for q in range(buckets):
        pp_out[:, pl.ds(q * TS, TS)] = potential[q : q + 1, :]

    spot_row = (lagr_in[...]) // TS
    moves = []
    for m in range(3):
        shift = (sums[m * buckets : (m + 1) * buckets, :] / s0 - xs[m]) * (1.0 / SCALE)
        hi = shift.astype(BF16).astype(F32)
        moves.append((hi, shift - hi))
    placed = jnp.zeros((6 * buckets, TS), F32)
    rows16 = iota((buckets, TS), 0)
    for q in range(buckets):
        on = spot_row[:, q * TS : (q + 1) * TS] == rows16
        stack = [
            jnp.where(on, part[q : q + 1, :], 0.0).astype(BF16) for pair in moves for part in pair
        ]
        placed = placed + jnp.dot(
            jnp.concatenate(stack, axis=0), hot_l[q], preferred_element_type=F32
        )
    for m in range(3):
        base = 2 * m * buckets
        field[m] = placed[base : base + buckets, :] + placed[base + buckets : base + 2 * buckets, :]

    edge = buckets - LB
    sends = [
        (field.at[0, pl.ds(edge, LB)], halo.at[0, pl.ds(0, LB)], (me, right)),
        (field.at[0, pl.ds(0, LB)], halo.at[1, pl.ds(0, LB)], (me, left)),
        (field.at[1], halo.at[2], (up, sl)),
        (field.at[1], halo.at[3], (down, sl)),
    ]
    copies = [
        pltpu.make_async_remote_copy(
            src_ref=src, dst_ref=dst, send_sem=hsem.at[0, i], recv_sem=hsem.at[1, i],
            device_id=device, device_id_type=MESH,
        )
        for i, (src, dst, device) in enumerate(sends)
    ]
    for copy in copies:
        copy.start()
    f2 = field[2]
    lanes = iota((buckets, TS), 1)
    third = jnp.where(lanes == TS - 1, 0.0, pltpu.roll(f2, TS - 1, 1)) - jnp.where(
        lanes == 0, 0.0, pltpu.roll(f2, 1, 1)
    )
    for copy in copies:
        copy.wait()
    f0, f1 = field[0], field[1]
    before = jnp.where(sl > 0, halo[0, 0:LB, :], 0.0)
    after = jnp.where(sl < ns - 1, halo[1, 0:LB, :], 0.0)
    first = jnp.concatenate([f0[LB:], after], axis=0) - jnp.concatenate([before, f0[:edge]], axis=0)
    below = jnp.where(me > 0, halo[2], 0.0)
    above = jnp.where(me < nb - 1, halo[3], 0.0)
    inner = lax.rem(rows16, LB)
    plus = jnp.where(inner == LB - 1, pltpu.roll(above, LB - 1, 0), pltpu.roll(f1, buckets - 1, 0))
    minus = jnp.where(inner == 0, pltpu.roll(below, buckets - (LB - 1), 0), pltpu.roll(f1, 1, 0))
    result = 0.5 * first + 0.5 * (plus - minus)
    result = result + 0.5 * third
    for a in range(buckets // LB):
        div_out[a] = result[a * LB : (a + 1) * LB, :]

    wait_sent(ask, 0)
    wait_sent(pay, 1)
    for sweep in range(ITERS):
        wait_sent(wsend.at[sweep], 2 + 2 * sweep)
        wait_sent(vsend.at[sweep], 3 + 2 * sweep)


def solution(mesh):
    nb, ns = mesh.shape["bricks"], mesh.shape["slab"]

    def on_device(
        part_pos, part_mass, cell_pos, cell_mass, cell_scale,
        req_tile, tile_bucket, tile_slot, tile_count, lagr_index,
    ):
        buckets, tiles = part_pos.shape[2] // TS, cell_pos.shape[2] // TS
        count = tile_bucket.shape[1]
        vmem = pl.BlockSpec(memory_space=pltpu.VMEM)
        smem = pl.BlockSpec(memory_space=pltpu.SMEM)
        return pl.pallas_call(
            functools.partial(kernel, nb, ns, buckets, tiles, count),
            out_shape=(
                jax.ShapeDtypeStruct((1, buckets * TS), F32),
                jax.ShapeDtypeStruct((1, tiles * TS), F32),
                jax.ShapeDtypeStruct((buckets // LB, LB, TS), F32),
            ),
            in_specs=[vmem] * 8 + [smem, vmem],
            out_specs=(vmem, vmem, vmem),
            scratch_shapes=[
                pltpu.VMEM((nb, TS), I32),
                pltpu.VMEM((nb, TS), I32),
                pltpu.VMEM((8, TL), I32),
                pltpu.SMEM((8, TL), I32),
                pltpu.VMEM((3, buckets, TS), F32),
                pltpu.VMEM((3, tiles, TS), F32),
                pltpu.VMEM((3, tiles, TS), F32),
                pltpu.VMEM((3, buckets, TS, TS), F32),
                pltpu.VMEM((buckets, TS, TS), F32),
                pltpu.VMEM((buckets, TS, TS), F32),
                pltpu.VMEM((count, TS, TS), F32),
                pltpu.VMEM((count, TS, TS), F32),
                pltpu.VMEM((count, 8, TS), F32),
                pltpu.VMEM((nb, 4, TS), F32),
                pltpu.VMEM((nb, 4, TS), F32),
                pltpu.VMEM((ITERS, nb, TS), F32),
                pltpu.VMEM((ITERS, nb, TS), F32),
                pltpu.VMEM((ITERS, nb, TS), F32),
                pltpu.VMEM((ITERS, nb, TS), F32),
                pltpu.VMEM((3, nb, TS), F32),
                pltpu.VMEM((buckets, TS, TS), BF16),
                pltpu.VMEM((3, buckets, TS), F32),
                pltpu.VMEM((4, buckets, TS), F32),
                pltpu.SemaphoreType.DMA((2 + 2 * ITERS,)),
                pltpu.SemaphoreType.DMA((2 + 2 * ITERS,)),
                pltpu.SemaphoreType.DMA((2, 4)),
                pltpu.SemaphoreType.DMA,
            ],
            name="sinkhorn",
            compiler_params=pltpu.CompilerParams(
                collective_id=0, has_side_effects=True, vmem_limit_bytes=56 << 20
            ),
        )(
            part_pos, part_mass, cell_pos, cell_mass, cell_scale,
            req_tile, tile_bucket, tile_slot, tile_count, lagr_index,
        )

    device = P(("bricks", "slab"))
    return jax.shard_map(
        on_device,
        mesh=mesh,
        in_specs=(device,) * 10,
        out_specs=(device, device, P("slab", "bricks", None)),
        check_vma=False,
    )
```

```python
import functools
import math

import jax
import jax.numpy as jnp
from jax import lax
from jax.experimental import pallas as pl
from jax.experimental.pallas import tpu as pltpu
from jax.sharding import PartitionSpec as P

TS = 128
EPS = 0.05
ITERS = 2
LB = 4
SCALE = math.sqrt(2.0 / (EPS * math.log(2.0)))
CENTER = (0.125, 0.125, 0.5)
HALF_LN2 = 0.5 * math.log(2.0)
MESH = pl.DeviceIdType.MESH
F32, BF16, I32 = jnp.float32, jnp.bfloat16, jnp.int32
TL = 256


def split3(a):
    hi = a.astype(BF16)
    rest = a - hi.astype(F32)
    mid = rest.astype(BF16)
    return hi, mid, (rest - mid.astype(F32)).astype(BF16)


def pick(hot, rows):
    hi, mid, lo = split3(rows)
    return jnp.dot(
        jnp.concatenate([hot, hot, hot], axis=1),
        jnp.concatenate([hi, mid, lo], axis=0),
        preferred_element_type=F32,
    )


def iota(shape, axis):
    return lax.broadcasted_iota(I32, shape, axis)


def kernel(
    nb, ns, buckets, tiles, count,
    pos_in, mass_in, cpos_in, cmass_in, cscale_in, req_in, tb_in, ts_in, cnt_in, lagr_in,
    out,
    ask, asked, lists_v, lists, xs, ys, rowsets, xb, mb, ub, kt, seg, colseg,
    offer, pay, cells, wsend, wrecv, vsend, vrecv, basis, turned, sums, hot_l, field, halo,
    ssem, rsem, hsem, lsem,
):
    me, sl = lax.axis_index("bricks"), lax.axis_index("slab")
    up, down = lax.rem(me + 1, nb), lax.rem(me + nb - 1, nb)
    right, left = lax.rem(sl + 1, ns), lax.rem(sl + ns - 1, ns)

    barrier = pltpu.get_barrier_semaphore()

    def greet(k, carry):
        pl.semaphore_signal(
            barrier, inc=1, device_id=(lax.rem(me + k, nb), sl), device_id_type=MESH
        )
        return carry

    lax.fori_loop(1, nb, greet, 0)
    for other in (left, right):
        pl.semaphore_signal(barrier, inc=1, device_id=(me, other), device_id_type=MESH)

    core, z, y = lax.rem(me, 2), lax.rem(me // 2, 8), me // 16

    def send_all(src, dst, phase):
        def one(k, carry):
            turn_z, turn_y = k // 8, lax.rem(k // 2, 4)
            step_z = 4 + (turn_z + 1) // 2 * (1 - 2 * lax.rem(turn_z, 2))
            step_y = 2 + (turn_y + 1) // 2 * (1 - 2 * lax.rem(turn_y, 2))
            peer = lax.rem(y + step_y, 4) * 16 + lax.rem(z + step_z, 8) * 2 + lax.rem(core + k + 1, 2)
            pltpu.make_async_remote_copy(
                src_ref=src.at[peer], dst_ref=dst.at[me],
                send_sem=ssem.at[phase], recv_sem=rsem.at[phase],
                device_id=(peer, sl), device_id_type=MESH,
            ).start()
            return carry

        lax.fori_loop(0, nb - 1, one, 0)
        pltpu.make_async_copy(src.at[me], dst.at[me], rsem.at[phase]).start()

    def wait_all(dst, phase):
        pltpu.make_async_copy(dst, dst, rsem.at[phase]).wait()

    def wait_sent(src, phase):
        part = src.at[pl.ds(0, nb - 1)]
        pltpu.make_async_copy(part, part, ssem.at[phase]).wait()

    ask[...] = jnp.broadcast_to(req_in[...], (TS, nb)).T

    lane = iota((1, TL), 1)
    live = lane < cnt_in[0]
    tb = jnp.concatenate([tb_in[...], jnp.zeros((1, TL - count), I32)], axis=1)
    ts = jnp.concatenate([ts_in[...], jnp.zeros((1, TL - count), I32)], axis=1)
    key_b = jnp.where(live, tb, buckets)
    key_s = jnp.where(live, ts, nb)
    uni_b, uni_s = key_b * TL + lane, key_s * TL + lane
    zero = jnp.zeros((1, TL), I32)
    cols = jnp.concatenate([uni_b, uni_s, tb, ts, key_b, key_s, zero, zero], axis=0).T
    col_tb, col_ts, col_kb, col_ks = (cols[:, i : i + 1] for i in range(2, 6))

    def total(where, value):
        return jnp.sum(jnp.where(where, value, 0), axis=0, keepdims=True)

    rank_b = total(cols[:, 0:1] < uni_b, 1)
    rank_s = total(cols[:, 1:2] < uni_s, 1)
    ranks = jnp.concatenate([rank_b, rank_s] + [zero] * 6, axis=0).T
    wide = iota((TL, TL), 1)
    at_b, at_s = ranks[:, 0:1] == wide, ranks[:, 1:2] == wide

    def same(row):
        return jnp.where((row == pltpu.roll(row, 1, 1)) & (lane > 0), 1, 0)

    def within(row, most):
        return jnp.minimum(jnp.maximum(row, 0), most)

    lists_v[0:1, :] = within(total(at_b, col_tb), buckets - 1)
    lists_v[1:2, :] = within(total(at_b, col_ts), nb - 1)
    lists_v[2:3, :] = same(total(at_b, col_kb))
    lists_v[3:4, :] = within(total(at_s, ranks[:, 0:1]), count - 1)
    lists_v[4:5, :] = within(total(at_s, col_tb), buckets - 1)
    lists_v[5:6, :] = same(total(at_s, col_ks))
    lists_v[6:7, :] = within(total(col_kb <= wide, 1) - 1, count - 1)
    lists_v[7:8, :] = within(total(col_ks <= wide, 1) - 1, count - 1)
    to_smem = pltpu.make_async_copy(lists_v, lists, lsem)
    to_smem.start()

    for q in range(buckets):
        part = pl.ds(q * TS, TS)
        rowsets[0, q : q + 1, :] = mass_in[:, part]
        for m in range(3):
            xs[m, q : q + 1, :] = (pos_in[m, :, part] - CENTER[m]) * SCALE
    for q in range(tiles):
        part = pl.ds(q * TS, TS)
        rowsets[1, q : q + 1, :] = cmass_in[:, part]
        rowsets[2, q : q + 1, :] = cscale_in[:, part]
        for m in range(3):
            ys[m, q : q + 1, :] = (cpos_in[m, :, part] - CENTER[m]) * SCALE
    ysq = ys[0] * ys[0] + ys[1] * ys[1] + ys[2] * ys[2]
    scaled = rowsets[2] * jnp.exp2(-0.5 * ysq)
    offer[...] = jnp.concatenate(split3(jnp.concatenate([ys[0], ys[1], ys[2], scaled], axis=1)), axis=0)

    pl.semaphore_wait(barrier, nb + 1)
    send_all(ask, asked, 0)

    columns = jnp.concatenate([xs[0], xs[1], xs[2], rowsets[0]], axis=0).T
    for q in range(buckets):
        for m in range(3):
            xb[m, q] = jnp.broadcast_to(columns[:, m * buckets + q : m * buckets + q + 1], (TS, TS))
        mb[q] = jnp.broadcast_to(columns[:, 3 * buckets + q : 3 * buckets + q + 1], (TS, TS))

    spots = jnp.concatenate(
        [lagr_in[:, pl.ds(q * TS, TS)] for q in range(buckets)] + [jnp.zeros((TS - buckets, TS), I32)], axis=0
    )
    spots_c = (spots & (TS - 1)).T
    for q in range(buckets):
        hot_l[pl.ds(q * TS, TS), :] = jnp.where(
            spots_c[:, q : q + 1] == iota((TS, TS), 1), 1.0, 0.0
        ).astype(BF16)

    wait_all(asked, 0)
    asks = asked[...].astype(F32)
    hot = jnp.where(asks[:, 0:tiles] == iota((nb, tiles), 1).astype(F32), 1.0, 0.0).astype(BF16)
    chosen = jnp.dot(jnp.concatenate([hot, hot, hot], axis=1), offer[...], preferred_element_type=F32)
    for m in range(4):
        pay[:, m, :] = chosen[:, m * TS : (m + 1) * TS]
    send_all(pay, cells, 1)
    cmass_of = pick(hot, rowsets[1])
    asks_t = asks.T
    twins = jnp.where(asks[:, 0:nb] == asks_t[0:nb, :], 1.0, 0.0).astype(BF16)
    hot_t = jnp.where(asks_t[0:tiles, :] == iota((tiles, nb), 0).astype(F32), 1.0, 0.0).astype(BF16)

    to_smem.wait()
    wait_all(cells, 1)

    def build(k, total):
        b, s = lists[0, k], lists[1, k]
        exponent = xb[0, b] * cells[s, 0:1] + xb[1, b] * cells[s, 1:2] + xb[2, b] * cells[s, 2:3]
        tile = jnp.exp2(exponent)
        kt[k] = tile
        total = jnp.where(lists[2, k] > 0, total, 0.0) + tile * cells[s, 3:4]
        seg[k] = total
        return total

    lax.fori_loop(0, count, build, jnp.zeros((TS, TS), F32), unroll=8)

    def row_pass(value):
        def step(k, total):
            total = jnp.where(lists[2, k] > 0, total, 0.0) + kt[k] * value(lists[1, k])
            seg[k] = total
            return total

        lax.fori_loop(0, count, step, jnp.zeros((TS, TS), F32), unroll=8)

    def col_pass(phase):
        def scale(q, carry):
            ub[q] = mb[q] / jnp.sum(seg[lists[6, q]], axis=1, keepdims=True)
            return carry

        lax.fori_loop(0, buckets, scale, 0, unroll=8)

        def step(k, total):
            product = kt[lists[3, k]] * ub[lists[4, k]]
            part = jnp.sum(product.reshape(TS // 8, 8, TS), axis=0)
            total = jnp.where(lists[5, k] > 0, total, 0.0) + part
            colseg[k] = total
            return total

        lax.fori_loop(0, count, step, jnp.zeros((8, TS), F32), unroll=8)

        def gather(s, carry):
            wsend[phase, pl.ds(s, 1), :] = jnp.sum(colseg[lists[7, s]], axis=0, keepdims=True)
            return carry

        lax.fori_loop(0, nb, gather, 0, unroll=8)

    def turn(quarter):
        def step(k, carry):
            flat = kt[k].T
            hi = flat.astype(BF16)
            turned[k, 0:TS, :] = hi
            turned[k, TS : 2 * TS, :] = (flat - hi.astype(F32)).astype(BF16)
            return carry

        lax.fori_loop(quarter * count // 4, (quarter + 1) * count // 4, step, 0, unroll=4)

    for sweep in range(ITERS):
        if sweep:
            row_pass(lambda s: vrecv[0, pl.ds(s, 1), :])
        col_pass(sweep)
        send_all(wsend.at[sweep], wrecv.at[sweep], 2 + 2 * sweep)
        turn(2 * sweep)
        wait_all(wrecv.at[sweep], 2 + 2 * sweep)
        vsend[sweep] = cmass_of / pick(twins, wrecv[sweep])
        send_all(vsend.at[sweep], vrecv.at[sweep], 3 + 2 * sweep)
        turn(2 * sweep + 1)
        if sweep == 0:
            for half in range(2):
                for m in range(3):
                    basis[:, 4 * half + m, :] = cells[:, m, :]
                basis[:, 4 * half + 3, :] = jnp.ones((nb, TS), F32)
        if sweep == ITERS - 1:
            cell_v = rowsets[1] / pick(hot_t, wrecv[sweep])
            potential = jnp.log(cell_v) + HALF_LN2 * ysq
            out[1] = potential
        wait_all(vrecv.at[sweep], 3 + 2 * sweep)

    upper = iota((8, TS), 0) < 4

    def last_step(k, total):
        s = lists[1, k]
        value = basis[s] * vrecv[ITERS - 1, pl.ds(s, 1), :]
        hi = value.astype(BF16).astype(F32)
        left_side = jnp.where(upper, hi, value - hi).astype(BF16)
        part = jnp.dot(
            jnp.concatenate([left_side, left_side], axis=1), turned[k], preferred_element_type=F32
        )
        total = jnp.where(lists[2, k] > 0, total, 0.0) + part
        colseg[k] = total
        return total

    lax.fori_loop(0, count, last_step, jnp.zeros((8, TS), F32), unroll=16)
    for q in range(buckets):
        both = colseg[lists[6, q]]
        both = both[0:4, :] + both[4:8, :]
        for m in range(4):
            sums[m, q : q + 1, :] = both[m : m + 1, :]
    s0 = sums[3]

    spot_row = lagr_in[...] // TS
    rows16 = iota((buckets, TS), 0)
    masks = [spot_row[:, q * TS : (q + 1) * TS] == rows16 for q in range(buckets)]

    def placed(axes):
        stack = []
        for m in axes:
            shift = (sums[m] / s0 - xs[m]) * (1.0 / SCALE)
            hi = shift.astype(BF16).astype(F32)
            for part in (hi, shift - hi):
                stack.append(
                    jnp.concatenate(
                        [
                            jnp.where(masks[q], part[q : q + 1, :], 0.0).astype(BF16)
                            for q in range(buckets)
                        ],
                        axis=1,
                    )
                )
        both = jnp.dot(jnp.concatenate(stack, axis=0), hot_l[...], preferred_element_type=F32)
        return [
            both[2 * i * buckets : (2 * i + 1) * buckets, :]
            + both[(2 * i + 1) * buckets : (2 * i + 2) * buckets, :]
            for i in range(len(axes))
        ]

    field[0], field[1] = placed((0, 1))
    edge = buckets - LB
    sends = [
        (field.at[0, pl.ds(edge, LB)], halo.at[0, pl.ds(0, LB)], (me, right)),
        (field.at[0, pl.ds(0, LB)], halo.at[1, pl.ds(0, LB)], (me, left)),
        (field.at[1], halo.at[2], (up, sl)),
        (field.at[1], halo.at[3], (down, sl)),
    ]
    copies = [
        pltpu.make_async_remote_copy(
            src_ref=src, dst_ref=dst, send_sem=hsem.at[0, i], recv_sem=hsem.at[1, i],
            device_id=device, device_id_type=MESH,
        )
        for i, (src, dst, device) in enumerate(sends)
    ]
    for copy in copies:
        copy.start()
    xsq = xs[0] * xs[0] + xs[1] * xs[1] + xs[2] * xs[2]
    potential = jnp.log(rowsets[0] / s0) + HALF_LN2 * xsq
    out[0] = potential
    (f2,) = placed((2,))
    lanes = iota((buckets, TS), 1)
    third = jnp.where(lanes == TS - 1, 0.0, pltpu.roll(f2, TS - 1, 1)) - jnp.where(
        lanes == 0, 0.0, pltpu.roll(f2, 1, 1)
    )
    for copy in copies:
        copy.wait()
    f0, f1 = field[0], field[1]
    before = jnp.where(sl > 0, halo[0, 0:LB, :], 0.0)
    after = jnp.where(sl < ns - 1, halo[1, 0:LB, :], 0.0)
    first = jnp.concatenate([f0[LB:], after], axis=0) - jnp.concatenate([before, f0[:edge]], axis=0)
    below = jnp.where(me > 0, halo[2], 0.0)
    above = jnp.where(me < nb - 1, halo[3], 0.0)
    inner = lax.rem(rows16, LB)
    plus = jnp.where(inner == LB - 1, pltpu.roll(above, LB - 1, 0), pltpu.roll(f1, buckets - 1, 0))
    minus = jnp.where(inner == 0, pltpu.roll(below, buckets - (LB - 1), 0), pltpu.roll(f1, 1, 0))
    result = 0.5 * first + 0.5 * (plus - minus)
    out[2] = result + 0.5 * third

    wait_sent(ask, 0)
    wait_sent(pay, 1)
    for sweep in range(ITERS):
        wait_sent(wsend.at[sweep], 2 + 2 * sweep)
        wait_sent(vsend.at[sweep], 3 + 2 * sweep)


def solution(mesh):
    nb, ns = mesh.shape["bricks"], mesh.shape["slab"]

    def on_device(
        part_pos, part_mass, cell_pos, cell_mass, cell_scale,
        req_tile, tile_bucket, tile_slot, tile_count, lagr_index,
    ):
        buckets, tiles = part_pos.shape[2] // TS, cell_pos.shape[2] // TS
        count = tile_bucket.shape[1]
        vmem = pl.BlockSpec(memory_space=pltpu.VMEM)
        smem = pl.BlockSpec(memory_space=pltpu.SMEM)
        out = pl.pallas_call(
            functools.partial(kernel, nb, ns, buckets, tiles, count),
            out_shape=jax.ShapeDtypeStruct((3, buckets, TS), F32),
            in_specs=[vmem] * 8 + [smem, vmem],
            out_specs=vmem,
            scratch_shapes=[
                pltpu.VMEM((nb, TS), I32),
                pltpu.VMEM((nb, TS), I32),
                pltpu.VMEM((8, TL), I32),
                pltpu.SMEM((8, TL), I32),
                pltpu.VMEM((3, buckets, TS), F32),
                pltpu.VMEM((3, tiles, TS), F32),
                pltpu.VMEM((3, tiles, TS), F32),
                pltpu.VMEM((3, buckets, TS, TS), F32),
                pltpu.VMEM((buckets, TS, TS), F32),
                pltpu.VMEM((buckets, TS, TS), F32),
                pltpu.VMEM((count, TS, TS), F32),
                pltpu.VMEM((count, TS, TS), F32),
                pltpu.VMEM((count, 8, TS), F32),
                pltpu.VMEM((3 * tiles, 4 * TS), BF16),
                pltpu.VMEM((nb, 4, TS), F32),
                pltpu.VMEM((nb, 4, TS), F32),
                pltpu.VMEM((ITERS, nb, TS), F32),
                pltpu.VMEM((ITERS, nb, TS), F32),
                pltpu.VMEM((ITERS, nb, TS), F32),
                pltpu.VMEM((ITERS, nb, TS), F32),
                pltpu.VMEM((nb, 8, TS), F32),
                pltpu.VMEM((count, 2 * TS, TS), BF16),
                pltpu.VMEM((4, buckets, TS), F32),
                pltpu.VMEM((buckets * TS, TS), BF16),
                pltpu.VMEM((2, buckets, TS), F32),
                pltpu.VMEM((4, buckets, TS), F32),
                pltpu.SemaphoreType.DMA((2 + 2 * ITERS,)),
                pltpu.SemaphoreType.DMA((2 + 2 * ITERS,)),
                pltpu.SemaphoreType.DMA((2, 4)),
                pltpu.SemaphoreType.DMA,
            ],
            name="sinkhorn",
            compiler_params=pltpu.CompilerParams(
                collective_id=0, has_side_effects=True, vmem_limit_bytes=56 << 20
            ),
        )(
            part_pos.transpose(1, 0, 2), part_mass, cell_pos.transpose(1, 0, 2), cell_mass, cell_scale,
            req_tile.T, tile_bucket, tile_slot, tile_count, lagr_index,
        )
        return out[0].reshape(1, -1), out[1].reshape(1, -1), out[2].reshape(-1, LB, TS)

    device = P(("bricks", "slab"))
    return jax.shard_map(
        on_device,
        mesh=mesh,
        in_specs=(device,) * 10,
        out_specs=(device, device, P("slab", "bricks", None)),
        check_vma=False,
    )
```

```python
import functools
import math

import jax
import jax.numpy as jnp
from jax import lax
from jax.experimental import pallas as pl
from jax.experimental.pallas import tpu as pltpu
from jax.sharding import PartitionSpec as P

TS = 128
EPS = 0.05
ITERS = 2
LB = 4
SCALE = math.sqrt(2.0 / (EPS * math.log(2.0)))
CENTER = (0.125, 0.125, 0.5)
HALF_LN2 = 0.5 * math.log(2.0)
MESH = pl.DeviceIdType.MESH
F32, BF16, I32 = jnp.float32, jnp.bfloat16, jnp.int32
TL = 256


def split3(a):
    hi = a.astype(BF16)
    rest = a - hi.astype(F32)
    mid = rest.astype(BF16)
    return hi, mid, (rest - mid.astype(F32)).astype(BF16)


def pick(hot, rows):
    hi, mid, lo = split3(rows)
    return jnp.dot(
        jnp.concatenate([hot, hot, hot], axis=1),
        jnp.concatenate([hi, mid, lo], axis=0),
        preferred_element_type=F32,
    )


def iota(shape, axis):
    return lax.broadcasted_iota(I32, shape, axis)


def kernel(
    nb, ns, buckets, tiles, count,
    pos_in, mass_in, cpos_in, cmass_in, cscale_in, req_in, tb_in, ts_in, cnt_in, lagr_in,
    out,
    ask, asked, lists_v, lists, xs, ys, rowsets, xb, mb, ub, kt, seg, colseg,
    offer, pay, cells, wsend, wrecv, vsend, vrecv, basis, turned, sums, hot_l, field, halo,
    ssem, rsem, hsem, lsem,
):
    me, sl = lax.axis_index("bricks"), lax.axis_index("slab")
    up, down = lax.rem(me + 1, nb), lax.rem(me + nb - 1, nb)
    right, left = lax.rem(sl + 1, ns), lax.rem(sl + ns - 1, ns)

    core, z, y = lax.rem(me, 2), lax.rem(me // 2, 8), me // 16

    def peer_at(k):
        turn_z, turn_y = k // 8, lax.rem(k // 2, 4)
        step_z = 4 + (turn_z + 1) // 2 * (1 - 2 * lax.rem(turn_z, 2))
        step_y = 2 + (turn_y + 1) // 2 * (1 - 2 * lax.rem(turn_y, 2))
        return lax.rem(y + step_y, 4) * 16 + lax.rem(z + step_z, 8) * 2 + lax.rem(core + k + 1, 2)

    def place_of(slot):
        def turn(step):
            return jnp.where(step < 0, -2 * step - 1, 2 * step)

        off_y = (((slot >> 4) + (4 - y)) & 3) - 2
        off_z = ((((slot >> 1) & 7) + (8 - z)) & 7) - 4
        off_core = ((slot & 1) + (2 - core)) & 1
        return turn(off_z) * 8 + turn(off_y) * 2 + 1 - off_core

    barrier = pltpu.get_barrier_semaphore()

    def greet(k, carry):
        pl.semaphore_signal(barrier, inc=1, device_id=(peer_at(k), sl), device_id_type=MESH)
        return carry

    lax.fori_loop(0, nb - 1, greet, 0, unroll=7)
    for other in (left, right):
        pl.semaphore_signal(barrier, inc=1, device_id=(me, other), device_id_type=MESH)

    def send_all(src, dst, phase):
        def one(k, carry):
            peer = peer_at(k)
            pltpu.make_async_remote_copy(
                src_ref=src.at[peer], dst_ref=dst.at[me],
                send_sem=ssem.at[phase], recv_sem=rsem.at[phase],
                device_id=(peer, sl), device_id_type=MESH,
            ).start()
            return carry

        lax.fori_loop(0, nb - 1, one, 0, unroll=7)
        pltpu.make_async_copy(src.at[me], dst.at[me], rsem.at[phase]).start()

    def wait_all(dst, phase):
        pltpu.make_async_copy(dst, dst, rsem.at[phase]).wait()

    def wait_sent(src, phase):
        part = src.at[pl.ds(0, nb - 1)]
        pltpu.make_async_copy(part, part, ssem.at[phase]).wait()

    ask[...] = jnp.broadcast_to(req_in[...], (TS, nb)).T

    lane = iota((1, TL), 1)
    live = lane < cnt_in[0]
    tb = jnp.concatenate([tb_in[...], jnp.zeros((1, TL - count), I32)], axis=1)
    ts = jnp.concatenate([ts_in[...], jnp.zeros((1, TL - count), I32)], axis=1)
    key_b = jnp.where(live, tb, buckets)
    key_s = jnp.where(live, place_of(ts), nb)
    uni_b, uni_s = key_b * TL + lane, key_s * TL + lane
    zero = jnp.zeros((1, TL), I32)
    cols = jnp.concatenate([uni_b, uni_s, tb, ts, key_b, key_s, zero, zero], axis=0).T
    col_tb, col_ts, col_kb, col_ks = (cols[:, i : i + 1] for i in range(2, 6))

    def total(where, value):
        return jnp.sum(jnp.where(where, value, 0), axis=0, keepdims=True)

    rank_b = total(cols[:, 0:1] < uni_b, 1)
    rank_s = total(cols[:, 1:2] < uni_s, 1)
    ranks = jnp.concatenate([rank_b, rank_s] + [zero] * 6, axis=0).T
    wide = iota((TL, TL), 1)
    at_b, at_s = ranks[:, 0:1] == wide, ranks[:, 1:2] == wide

    def same(row):
        return jnp.where((row == pltpu.roll(row, 1, 1)) & (lane > 0), 1, 0)

    def within(row, most):
        return jnp.minimum(jnp.maximum(row, 0), most)

    lists_v[0:1, :] = within(total(at_b, col_tb), buckets - 1)
    lists_v[1:2, :] = within(total(at_b, col_ts), nb - 1)
    lists_v[2:3, :] = same(total(at_b, col_kb))
    lists_v[3:4, :] = within(total(at_s, ranks[:, 0:1]), count - 1)
    lists_v[4:5, :] = within(total(at_s, col_tb), buckets - 1)
    lists_v[5:6, :] = same(total(at_s, col_ks))
    lists_v[6:7, :] = within(total(col_kb <= wide, 1) - 1, count - 1)
    lists_v[7:8, :] = within(total(col_ks <= wide, 1) - 1, count - 1)
    to_smem = pltpu.make_async_copy(lists_v, lists, lsem)
    to_smem.start()

    for q in range(buckets):
        part = pl.ds(q * TS, TS)
        rowsets[0, q : q + 1, :] = mass_in[:, part]
        for m in range(3):
            xs[m, q : q + 1, :] = (pos_in[m, :, part] - CENTER[m]) * SCALE
    for q in range(tiles):
        part = pl.ds(q * TS, TS)
        rowsets[1, q : q + 1, :] = cmass_in[:, part]
        rowsets[2, q : q + 1, :] = cscale_in[:, part]
        for m in range(3):
            ys[m, q : q + 1, :] = (cpos_in[m, :, part] - CENTER[m]) * SCALE
    ysq = ys[0] * ys[0] + ys[1] * ys[1] + ys[2] * ys[2]
    scaled = rowsets[2] * jnp.exp2(-0.5 * ysq)
    offer[...] = jnp.concatenate(split3(jnp.concatenate([ys[0], ys[1], ys[2], scaled], axis=1)), axis=0)

    pl.semaphore_wait(barrier, nb + 1)
    send_all(ask, asked, 0)

    columns = jnp.concatenate([xs[0], xs[1], xs[2], rowsets[0]], axis=0).T
    for q in range(buckets):
        for m in range(3):
            xb[m, q] = jnp.broadcast_to(columns[:, m * buckets + q : m * buckets + q + 1], (TS, TS))
        mb[q] = jnp.broadcast_to(columns[:, 3 * buckets + q : 3 * buckets + q + 1], (TS, TS))

    spots = jnp.concatenate(
        [lagr_in[:, pl.ds(q * TS, TS)] for q in range(buckets)] + [jnp.zeros((TS - buckets, TS), I32)], axis=0
    )
    spots_c = (spots & (TS - 1)).T
    for q in range(buckets):
        hot_l[pl.ds(q * TS, TS), :] = jnp.where(
            spots_c[:, q : q + 1] == iota((TS, TS), 1), 1.0, 0.0
        ).astype(BF16)

    wait_all(asked, 0)
    asks = asked[...].astype(F32)
    hot = jnp.where(asks[:, 0:tiles] == iota((nb, tiles), 1).astype(F32), 1.0, 0.0).astype(BF16)
    chosen = jnp.dot(jnp.concatenate([hot, hot, hot], axis=1), offer[...], preferred_element_type=F32)
    for m in range(4):
        pay[:, m, :] = chosen[:, m * TS : (m + 1) * TS]
    send_all(pay, cells, 1)
    cmass_of = pick(hot, rowsets[1])
    asks_t = asks.T
    twins = jnp.where(asks[:, 0:nb] == asks_t[0:nb, :], 1.0, 0.0).astype(BF16)
    hot_t = jnp.where(asks_t[0:tiles, :] == iota((tiles, nb), 0).astype(F32), 1.0, 0.0).astype(BF16)

    to_smem.wait()
    wait_all(cells, 1)

    def build(k, total):
        b, s = lists[0, k], lists[1, k]
        exponent = xb[0, b] * cells[s, 0:1] + xb[1, b] * cells[s, 1:2] + xb[2, b] * cells[s, 2:3]
        tile = jnp.exp2(exponent)
        kt[k] = tile
        total = jnp.where(lists[2, k] > 0, total, 0.0) + tile * cells[s, 3:4]
        seg[k] = total
        return total

    lax.fori_loop(0, count, build, jnp.zeros((TS, TS), F32), unroll=8)

    def row_pass(value):
        def step(k, total):
            total = jnp.where(lists[2, k] > 0, total, 0.0) + kt[k] * value(lists[1, k])
            seg[k] = total
            return total

        lax.fori_loop(0, count, step, jnp.zeros((TS, TS), F32), unroll=8)

    def col_pass(sweep):
        def scale(q, carry):
            ub[q] = mb[q] / jnp.sum(seg[lists[6, q]], axis=1, keepdims=True)
            return carry

        lax.fori_loop(0, buckets, scale, 0, unroll=8)

        def step(k, total):
            product = kt[lists[3, k]] * ub[lists[4, k]]
            part = jnp.sum(product.reshape(TS // 8, 8, TS), axis=0)
            total = jnp.where(lists[5, k] > 0, total, 0.0) + part
            colseg[k] = total
            return total

        group = 8

        def steps_and_sends(block, total, sends):
            first = block * group
            for i in range(group):
                total = step(count - nb + first + i, total)
            for i in range(group):
                wsend[sweep, pl.ds(first + i, 1), :] = jnp.sum(
                    colseg[lists[7, first + i]], axis=0, keepdims=True
                )
            for i in range(sends):
                pltpu.make_async_remote_copy(
                    src_ref=wsend.at[sweep, first + i], dst_ref=wrecv.at[sweep, me],
                    send_sem=ssem.at[2 + 2 * sweep], recv_sem=rsem.at[2 + 2 * sweep],
                    device_id=(peer_at(first + i), sl), device_id_type=MESH,
                ).start()
            return total

        total = lax.fori_loop(0, count - nb, step, jnp.zeros((8, TS), F32), unroll=8)
        total = lax.fori_loop(
            0, nb // group - 1, lambda block, carry: steps_and_sends(block, carry, group), total
        )
        steps_and_sends(nb // group - 1, total, group - 1)
        pltpu.make_async_copy(
            wsend.at[sweep, nb - 1], wrecv.at[sweep, me], rsem.at[2 + 2 * sweep]
        ).start()

    def turn(quarter):
        def step(k, carry):
            flat = kt[k].T
            hi = flat.astype(BF16)
            turned[k, 0:TS, :] = hi
            turned[k, TS : 2 * TS, :] = (flat - hi.astype(F32)).astype(BF16)
            return carry

        lax.fori_loop(quarter * count // 4, (quarter + 1) * count // 4, step, 0, unroll=4)

    for sweep in range(ITERS):
        if sweep:
            row_pass(lambda s: vrecv[0, pl.ds(s, 1), :])
        col_pass(sweep)
        turn(2 * sweep)
        wait_all(wrecv.at[sweep], 2 + 2 * sweep)
        vsend[sweep] = cmass_of / pick(twins, wrecv[sweep])
        send_all(vsend.at[sweep], vrecv.at[sweep], 3 + 2 * sweep)
        turn(2 * sweep + 1)
        if sweep == 0:
            for half in range(2):
                for m in range(3):
                    basis[:, 4 * half + m, :] = cells[:, m, :]
                basis[:, 4 * half + 3, :] = jnp.ones((nb, TS), F32)
        if sweep == ITERS - 1:
            cell_v = rowsets[1] / pick(hot_t, wrecv[sweep])
            potential = jnp.log(cell_v) + HALF_LN2 * ysq
            out[1] = potential
        wait_all(vrecv.at[sweep], 3 + 2 * sweep)

    upper = iota((8, TS), 0) < 4

    def last_step(k, total):
        s = lists[1, k]
        value = basis[s] * vrecv[ITERS - 1, pl.ds(s, 1), :]
        hi = value.astype(BF16).astype(F32)
        left_side = jnp.where(upper, hi, value - hi).astype(BF16)
        part = jnp.dot(
            jnp.concatenate([left_side, left_side], axis=1), turned[k], preferred_element_type=F32
        )
        total = jnp.where(lists[2, k] > 0, total, 0.0) + part
        colseg[k] = total
        return total

    lax.fori_loop(0, count, last_step, jnp.zeros((8, TS), F32), unroll=36)
    for q in range(buckets):
        both = colseg[lists[6, q]]
        both = both[0:4, :] + both[4:8, :]
        for m in range(4):
            sums[m, q : q + 1, :] = both[m : m + 1, :]
    s0 = sums[3]

    spot_row = lagr_in[...] // TS
    rows16 = iota((buckets, TS), 0)
    masks = [spot_row[:, q * TS : (q + 1) * TS] == rows16 for q in range(buckets)]

    def placed(axes):
        stack = []
        for m in axes:
            shift = (sums[m] / s0 - xs[m]) * (1.0 / SCALE)
            hi = shift.astype(BF16).astype(F32)
            for part in (hi, shift - hi):
                stack.append(
                    jnp.concatenate(
                        [
                            jnp.where(masks[q], part[q : q + 1, :], 0.0).astype(BF16)
                            for q in range(buckets)
                        ],
                        axis=1,
                    )
                )
        both = jnp.dot(jnp.concatenate(stack, axis=0), hot_l[...], preferred_element_type=F32)
        return [
            both[2 * i * buckets : (2 * i + 1) * buckets, :]
            + both[(2 * i + 1) * buckets : (2 * i + 2) * buckets, :]
            for i in range(len(axes))
        ]

    field[0], field[1] = placed((0, 1))
    edge = buckets - LB
    sends = [
        (field.at[0, pl.ds(edge, LB)], halo.at[0, pl.ds(0, LB)], (me, right)),
        (field.at[0, pl.ds(0, LB)], halo.at[1, pl.ds(0, LB)], (me, left)),
        (field.at[1], halo.at[2], (up, sl)),
        (field.at[1], halo.at[3], (down, sl)),
    ]
    copies = [
        pltpu.make_async_remote_copy(
            src_ref=src, dst_ref=dst, send_sem=hsem.at[0, i], recv_sem=hsem.at[1, i],
            device_id=device, device_id_type=MESH,
        )
        for i, (src, dst, device) in enumerate(sends)
    ]
    for copy in copies:
        copy.start()
    xsq = xs[0] * xs[0] + xs[1] * xs[1] + xs[2] * xs[2]
    potential = jnp.log(rowsets[0] / s0) + HALF_LN2 * xsq
    out[0] = potential
    (f2,) = placed((2,))
    lanes = iota((buckets, TS), 1)
    third = jnp.where(lanes == TS - 1, 0.0, pltpu.roll(f2, TS - 1, 1)) - jnp.where(
        lanes == 0, 0.0, pltpu.roll(f2, 1, 1)
    )
    for copy in copies:
        copy.wait()
    f0, f1 = field[0], field[1]
    before = jnp.where(sl > 0, halo[0, 0:LB, :], 0.0)
    after = jnp.where(sl < ns - 1, halo[1, 0:LB, :], 0.0)
    first = jnp.concatenate([f0[LB:], after], axis=0) - jnp.concatenate([before, f0[:edge]], axis=0)
    below = jnp.where(me > 0, halo[2], 0.0)
    above = jnp.where(me < nb - 1, halo[3], 0.0)
    inner = lax.rem(rows16, LB)
    plus = jnp.where(inner == LB - 1, pltpu.roll(above, LB - 1, 0), pltpu.roll(f1, buckets - 1, 0))
    minus = jnp.where(inner == 0, pltpu.roll(below, buckets - (LB - 1), 0), pltpu.roll(f1, 1, 0))
    result = 0.5 * first + 0.5 * (plus - minus)
    out[2] = result + 0.5 * third

    wait_sent(ask, 0)
    wait_sent(pay, 1)
    for sweep in range(ITERS):
        wait_sent(wsend.at[sweep], 2 + 2 * sweep)
        wait_sent(vsend.at[sweep], 3 + 2 * sweep)


def solution(mesh):
    nb, ns = mesh.shape["bricks"], mesh.shape["slab"]

    def on_device(
        part_pos, part_mass, cell_pos, cell_mass, cell_scale,
        req_tile, tile_bucket, tile_slot, tile_count, lagr_index,
    ):
        buckets, tiles = part_pos.shape[2] // TS, cell_pos.shape[2] // TS
        count = tile_bucket.shape[1]
        vmem = pl.BlockSpec(memory_space=pltpu.VMEM)
        smem = pl.BlockSpec(memory_space=pltpu.SMEM)
        out = pl.pallas_call(
            functools.partial(kernel, nb, ns, buckets, tiles, count),
            out_shape=jax.ShapeDtypeStruct((3, buckets, TS), F32),
            in_specs=[vmem] * 8 + [smem, vmem],
            out_specs=vmem,
            scratch_shapes=[
                pltpu.VMEM((nb, TS), I32),
                pltpu.VMEM((nb, TS), I32),
                pltpu.VMEM((8, TL), I32),
                pltpu.SMEM((8, TL), I32),
                pltpu.VMEM((3, buckets, TS), F32),
                pltpu.VMEM((3, tiles, TS), F32),
                pltpu.VMEM((3, tiles, TS), F32),
                pltpu.VMEM((3, buckets, TS, TS), F32),
                pltpu.VMEM((buckets, TS, TS), F32),
                pltpu.VMEM((buckets, TS, TS), F32),
                pltpu.VMEM((count, TS, TS), F32),
                pltpu.VMEM((count, TS, TS), F32),
                pltpu.VMEM((count, 8, TS), F32),
                pltpu.VMEM((3 * tiles, 4 * TS), BF16),
                pltpu.VMEM((nb, 4, TS), F32),
                pltpu.VMEM((nb, 4, TS), F32),
                pltpu.VMEM((ITERS, nb, TS), F32),
                pltpu.VMEM((ITERS, nb, TS), F32),
                pltpu.VMEM((ITERS, nb, TS), F32),
                pltpu.VMEM((ITERS, nb, TS), F32),
                pltpu.VMEM((nb, 8, TS), F32),
                pltpu.VMEM((count, 2 * TS, TS), BF16),
                pltpu.VMEM((4, buckets, TS), F32),
                pltpu.VMEM((buckets * TS, TS), BF16),
                pltpu.VMEM((2, buckets, TS), F32),
                pltpu.VMEM((4, buckets, TS), F32),
                pltpu.SemaphoreType.DMA((2 + 2 * ITERS,)),
                pltpu.SemaphoreType.DMA((2 + 2 * ITERS,)),
                pltpu.SemaphoreType.DMA((2, 4)),
                pltpu.SemaphoreType.DMA,
            ],
            name="sinkhorn",
            compiler_params=pltpu.CompilerParams(
                collective_id=0, has_side_effects=True, vmem_limit_bytes=56 << 20
            ),
        )(
            part_pos.transpose(1, 0, 2), part_mass, cell_pos.transpose(1, 0, 2), cell_mass, cell_scale,
            req_tile.T, tile_bucket, tile_slot, tile_count, lagr_index,
        )
        return out[0].reshape(1, -1), out[1].reshape(1, -1), out[2].reshape(-1, LB, TS)

    device = P(("bricks", "slab"))
    return jax.shard_map(
        on_device,
        mesh=mesh,
        in_specs=(device,) * 10,
        out_specs=(device, device, P("slab", "bricks", None)),
        check_vma=False,
    )
```

```python
import functools
import math

import jax
import jax.numpy as jnp
from jax import lax
from jax.experimental import pallas as pl
from jax.experimental.pallas import tpu as pltpu
from jax.sharding import PartitionSpec as P

TS = 128
EPS = 0.05
ITERS = 2
LB = 4
SCALE = math.sqrt(2.0 / (EPS * math.log(2.0)))
CENTER = (0.125, 0.125, 0.5)
HALF_LN2 = 0.5 * math.log(2.0)
MESH = pl.DeviceIdType.MESH
F32, BF16, I32 = jnp.float32, jnp.bfloat16, jnp.int32
TL = 256


def split3(a):
    hi = a.astype(BF16)
    rest = a - hi.astype(F32)
    mid = rest.astype(BF16)
    return hi, mid, (rest - mid.astype(F32)).astype(BF16)


def pick(hot, rows):
    hi, mid, lo = split3(rows)
    return jnp.dot(
        jnp.concatenate([hot, hot, hot], axis=1),
        jnp.concatenate([hi, mid, lo], axis=0),
        preferred_element_type=F32,
    )


def iota(shape, axis):
    return lax.broadcasted_iota(I32, shape, axis)


def kernel(
    nb, ns, buckets, tiles, count,
    pos_far, mass_far, cpos_far, cmass_far, cscale_far, req_far, tb_far, ts_far, cnt_in, lagr_far,
    out,
    pos_in, mass_in, cpos_in, cmass_in, cscale_in, req_in, tb_in, ts_in, lagr_in, isem,
    ask, asked, lists_v, lists, xs, ys, rowsets, xb, mb, ub, kt, seg, colseg,
    offer, pay, cells, wsend, wrecv, vsend, vrecv, basis, turned, sums, hot_l, field, halo,
    ssem, rsem, hsem, lsem,
):
    me, sl = lax.axis_index("bricks"), lax.axis_index("slab")
    up, down = lax.rem(me + 1, nb), lax.rem(me + nb - 1, nb)
    right, left = lax.rem(sl + 1, ns), lax.rem(sl + ns - 1, ns)

    core, z, y = lax.rem(me, 2), lax.rem(me // 2, 8), me // 16

    def peer_at(k):
        turn_z, turn_y = k // 8, lax.rem(k // 2, 4)
        step_z = 4 + (turn_z + 1) // 2 * (1 - 2 * lax.rem(turn_z, 2))
        step_y = 2 + (turn_y + 1) // 2 * (1 - 2 * lax.rem(turn_y, 2))
        return lax.rem(y + step_y, 4) * 16 + lax.rem(z + step_z, 8) * 2 + lax.rem(core + k + 1, 2)

    def place_of(slot):
        def turn(step):
            return jnp.where(step < 0, -2 * step - 1, 2 * step)

        off_y = (((slot >> 4) + (4 - y)) & 3) - 2
        off_z = ((((slot >> 1) & 7) + (8 - z)) & 7) - 4
        off_core = ((slot & 1) + (2 - core)) & 1
        return turn(off_z) * 8 + turn(off_y) * 2 + 1 - off_core

    barrier = pltpu.get_barrier_semaphore()

    def greet(k, carry):
        pl.semaphore_signal(barrier, inc=1, device_id=(peer_at(k), sl), device_id_type=MESH)
        return carry

    lax.fori_loop(0, nb - 1, greet, 0, unroll=7)
    for other in (left, right):
        pl.semaphore_signal(barrier, inc=1, device_id=(me, other), device_id_type=MESH)

    loads = [
        pltpu.make_async_copy(far, near, isem.at[i])
        for i, (far, near) in enumerate(
            (
                (req_far, req_in), (tb_far, tb_in), (ts_far, ts_in), (pos_far, pos_in),
                (mass_far, mass_in), (cpos_far, cpos_in), (cmass_far, cmass_in),
                (cscale_far, cscale_in), (lagr_far, lagr_in),
            )
        )
    ]
    for load in loads:
        load.start()

    def send_all(src, dst, phase):
        def one(k, carry):
            peer = peer_at(k)
            pltpu.make_async_remote_copy(
                src_ref=src.at[peer], dst_ref=dst.at[me],
                send_sem=ssem.at[phase], recv_sem=rsem.at[phase],
                device_id=(peer, sl), device_id_type=MESH,
            ).start()
            return carry

        lax.fori_loop(0, nb - 1, one, 0, unroll=7)
        pltpu.make_async_copy(src.at[me], dst.at[me], rsem.at[phase]).start()

    def wait_all(dst, phase):
        pltpu.make_async_copy(dst, dst, rsem.at[phase]).wait()

    def wait_sent(src, phase):
        part = src.at[pl.ds(0, nb - 1)]
        pltpu.make_async_copy(part, part, ssem.at[phase]).wait()

    for load in loads:
        load.wait()
    ask[...] = jnp.broadcast_to(req_in[...], (TS, nb)).T

    lane = iota((1, TL), 1)
    live = lane < cnt_in[0]
    tb = jnp.concatenate([tb_in[...], jnp.zeros((1, TL - count), I32)], axis=1)
    ts = jnp.concatenate([ts_in[...], jnp.zeros((1, TL - count), I32)], axis=1)
    key_b = jnp.where(live, tb, buckets)
    key_s = jnp.where(live, place_of(ts), nb)
    uni_b, uni_s = key_b * TL + lane, key_s * TL + lane
    zero = jnp.zeros((1, TL), I32)
    cols = jnp.concatenate([uni_b, uni_s, tb, ts, key_b, key_s, zero, zero], axis=0).T
    col_tb, col_ts, col_kb, col_ks = (cols[:, i : i + 1] for i in range(2, 6))

    def total(where, value):
        return jnp.sum(jnp.where(where, value, 0), axis=0, keepdims=True)

    rank_b = total(cols[:, 0:1] < uni_b, 1)
    rank_s = total(cols[:, 1:2] < uni_s, 1)
    ranks = jnp.concatenate([rank_b, rank_s] + [zero] * 6, axis=0).T
    wide = iota((TL, TL), 1)
    at_b, at_s = ranks[:, 0:1] == wide, ranks[:, 1:2] == wide

    def same(row):
        return jnp.where((row == pltpu.roll(row, 1, 1)) & (lane > 0), 1, 0)

    def within(row, most):
        return jnp.minimum(jnp.maximum(row, 0), most)

    lists_v[0:1, :] = within(total(at_b, col_tb), buckets - 1)
    lists_v[1:2, :] = within(total(at_b, col_ts), nb - 1)
    lists_v[2:3, :] = same(total(at_b, col_kb))
    lists_v[3:4, :] = within(total(at_s, ranks[:, 0:1]), count - 1)
    lists_v[4:5, :] = within(total(at_s, col_tb), buckets - 1)
    lists_v[5:6, :] = same(total(at_s, col_ks))
    lists_v[6:7, :] = within(total(col_kb <= wide, 1) - 1, count - 1)
    lists_v[7:8, :] = within(total(col_ks <= wide, 1) - 1, count - 1)
    to_smem = pltpu.make_async_copy(lists_v, lists, lsem)
    to_smem.start()

    for q in range(buckets):
        part = pl.ds(q * TS, TS)
        rowsets[0, q : q + 1, :] = mass_in[:, part]
        for m in range(3):
            xs[m, q : q + 1, :] = (pos_in[m, :, part] - CENTER[m]) * SCALE
    for q in range(tiles):
        part = pl.ds(q * TS, TS)
        rowsets[1, q : q + 1, :] = cmass_in[:, part]
        rowsets[2, q : q + 1, :] = cscale_in[:, part]
        for m in range(3):
            ys[m, q : q + 1, :] = (cpos_in[m, :, part] - CENTER[m]) * SCALE
    ysq = ys[0] * ys[0] + ys[1] * ys[1] + ys[2] * ys[2]
    scaled = rowsets[2] * jnp.exp2(-0.5 * ysq)
    offer[...] = jnp.concatenate(split3(jnp.concatenate([ys[0], ys[1], ys[2], scaled], axis=1)), axis=0)

    pl.semaphore_wait(barrier, nb + 1)
    send_all(ask, asked, 0)

    columns = jnp.concatenate([xs[0], xs[1], xs[2], rowsets[0]], axis=0).T
    for q in range(buckets):
        for m in range(3):
            xb[m, q] = jnp.broadcast_to(columns[:, m * buckets + q : m * buckets + q + 1], (TS, TS))
        mb[q] = jnp.broadcast_to(columns[:, 3 * buckets + q : 3 * buckets + q + 1], (TS, TS))

    spots = jnp.concatenate(
        [lagr_in[:, pl.ds(q * TS, TS)] for q in range(buckets)] + [jnp.zeros((TS - buckets, TS), I32)], axis=0
    )
    spots_c = (spots & (TS - 1)).T
    for q in range(buckets):
        hot_l[pl.ds(q * TS, TS), :] = jnp.where(
            spots_c[:, q : q + 1] == iota((TS, TS), 1), 1.0, 0.0
        ).astype(BF16)

    wait_all(asked, 0)
    asks = asked[...].astype(F32)
    hot = jnp.where(asks[:, 0:tiles] == iota((nb, tiles), 1).astype(F32), 1.0, 0.0).astype(BF16)
    chosen = jnp.dot(jnp.concatenate([hot, hot, hot], axis=1), offer[...], preferred_element_type=F32)
    for m in range(4):
        pay[:, m, :] = chosen[:, m * TS : (m + 1) * TS]
    send_all(pay, cells, 1)
    cmass_of = pick(hot, rowsets[1])
    asks_t = asks.T
    twins = jnp.where(asks[:, 0:nb] == asks_t[0:nb, :], 1.0, 0.0).astype(BF16)
    hot_t = jnp.where(asks_t[0:tiles, :] == iota((tiles, nb), 0).astype(F32), 1.0, 0.0).astype(BF16)

    to_smem.wait()
    wait_all(cells, 1)

    def build(k, total):
        b, s = lists[0, k], lists[1, k]
        exponent = xb[0, b] * cells[s, 0:1] + xb[1, b] * cells[s, 1:2] + xb[2, b] * cells[s, 2:3]
        tile = jnp.exp2(exponent)
        kt[k] = tile
        total = jnp.where(lists[2, k] > 0, total, 0.0) + tile * cells[s, 3:4]
        seg[k] = total
        return total

    lax.fori_loop(0, count, build, jnp.zeros((TS, TS), F32), unroll=8)

    def row_pass(value):
        def step(k, total):
            total = jnp.where(lists[2, k] > 0, total, 0.0) + kt[k] * value(lists[1, k])
            seg[k] = total
            return total

        lax.fori_loop(0, count, step, jnp.zeros((TS, TS), F32), unroll=8)

    def col_pass(sweep):
        def scale(q, carry):
            ub[q] = mb[q] / jnp.sum(seg[lists[6, q]], axis=1, keepdims=True)
            return carry

        lax.fori_loop(0, buckets, scale, 0, unroll=8)

        def step(k, total):
            product = kt[lists[3, k]] * ub[lists[4, k]]
            part = jnp.sum(product.reshape(TS // 8, 8, TS), axis=0)
            total = jnp.where(lists[5, k] > 0, total, 0.0) + part
            colseg[k] = total
            return total

        group = 8

        def steps_and_sends(block, total, sends):
            first = block * group
            for i in range(group):
                total = step(count - nb + first + i, total)
            for i in range(group):
                wsend[sweep, pl.ds(first + i, 1), :] = jnp.sum(
                    colseg[lists[7, first + i]], axis=0, keepdims=True
                )
            for i in range(sends):
                pltpu.make_async_remote_copy(
                    src_ref=wsend.at[sweep, first + i], dst_ref=wrecv.at[sweep, me],
                    send_sem=ssem.at[2 + 2 * sweep], recv_sem=rsem.at[2 + 2 * sweep],
                    device_id=(peer_at(first + i), sl), device_id_type=MESH,
                ).start()
            return total

        total = lax.fori_loop(0, count - nb, step, jnp.zeros((8, TS), F32), unroll=8)
        total = lax.fori_loop(
            0, nb // group - 1, lambda block, carry: steps_and_sends(block, carry, group), total
        )
        steps_and_sends(nb // group - 1, total, group - 1)
        pltpu.make_async_copy(
            wsend.at[sweep, nb - 1], wrecv.at[sweep, me], rsem.at[2 + 2 * sweep]
        ).start()

    def turn(quarter):
        def step(k, carry):
            flat = kt[k].T
            hi = flat.astype(BF16)
            turned[k, 0:TS, :] = hi
            turned[k, TS : 2 * TS, :] = (flat - hi.astype(F32)).astype(BF16)
            return carry

        lax.fori_loop(quarter * count // 4, (quarter + 1) * count // 4, step, 0, unroll=2)

    for sweep in range(ITERS):
        if sweep:
            row_pass(lambda s: vrecv[0, pl.ds(s, 1), :])
        col_pass(sweep)
        turn(2 * sweep)
        wait_all(wrecv.at[sweep], 2 + 2 * sweep)
        vsend[sweep] = cmass_of / pick(twins, wrecv[sweep])
        send_all(vsend.at[sweep], vrecv.at[sweep], 3 + 2 * sweep)
        turn(2 * sweep + 1)
        if sweep == 0:
            for half in range(2):
                for m in range(3):
                    basis[:, 4 * half + m, :] = cells[:, m, :]
                basis[:, 4 * half + 3, :] = jnp.ones((nb, TS), F32)
        if sweep == ITERS - 1:
            cell_v = rowsets[1] / pick(hot_t, wrecv[sweep])
            potential = jnp.log(cell_v) + HALF_LN2 * ysq
            out[1] = potential
        wait_all(vrecv.at[sweep], 3 + 2 * sweep)

    upper = iota((8, TS), 0) < 4

    def last_step(k, total):
        s = lists[1, k]
        value = basis[s] * vrecv[ITERS - 1, pl.ds(s, 1), :]
        hi = value.astype(BF16).astype(F32)
        left_side = jnp.where(upper, hi, value - hi).astype(BF16)
        part = jnp.dot(
            jnp.concatenate([left_side, left_side], axis=1), turned[k], preferred_element_type=F32
        )
        total = jnp.where(lists[2, k] > 0, total, 0.0) + part
        colseg[k] = total
        return total

    lax.fori_loop(0, count, last_step, jnp.zeros((8, TS), F32), unroll=36)
    for q in range(buckets):
        both = colseg[lists[6, q]]
        both = both[0:4, :] + both[4:8, :]
        for m in range(4):
            sums[m, q : q + 1, :] = both[m : m + 1, :]
    s0 = sums[3]

    spot_row = lagr_in[...] // TS
    rows16 = iota((buckets, TS), 0)
    masks = [spot_row[:, q * TS : (q + 1) * TS] == rows16 for q in range(buckets)]

    def placed(axes):
        stack = []
        for m in axes:
            shift = (sums[m] / s0 - xs[m]) * (1.0 / SCALE)
            hi = shift.astype(BF16).astype(F32)
            for part in (hi, shift - hi):
                stack.append(
                    jnp.concatenate(
                        [
                            jnp.where(masks[q], part[q : q + 1, :], 0.0).astype(BF16)
                            for q in range(buckets)
                        ],
                        axis=1,
                    )
                )
        both = jnp.dot(jnp.concatenate(stack, axis=0), hot_l[...], preferred_element_type=F32)
        return [
            both[2 * i * buckets : (2 * i + 1) * buckets, :]
            + both[(2 * i + 1) * buckets : (2 * i + 2) * buckets, :]
            for i in range(len(axes))
        ]

    field[0], field[1] = placed((0, 1))
    edge = buckets - LB
    sends = [
        (field.at[0, pl.ds(edge, LB)], halo.at[0, pl.ds(0, LB)], (me, right)),
        (field.at[0, pl.ds(0, LB)], halo.at[1, pl.ds(0, LB)], (me, left)),
        (field.at[1], halo.at[2], (up, sl)),
        (field.at[1], halo.at[3], (down, sl)),
    ]
    copies = [
        pltpu.make_async_remote_copy(
            src_ref=src, dst_ref=dst, send_sem=hsem.at[0, i], recv_sem=hsem.at[1, i],
            device_id=device, device_id_type=MESH,
        )
        for i, (src, dst, device) in enumerate(sends)
    ]
    for copy in copies:
        copy.start()
    xsq = xs[0] * xs[0] + xs[1] * xs[1] + xs[2] * xs[2]
    potential = jnp.log(rowsets[0] / s0) + HALF_LN2 * xsq
    out[0] = potential
    (f2,) = placed((2,))
    lanes = iota((buckets, TS), 1)
    third = jnp.where(lanes == TS - 1, 0.0, pltpu.roll(f2, TS - 1, 1)) - jnp.where(
        lanes == 0, 0.0, pltpu.roll(f2, 1, 1)
    )
    for copy in copies:
        copy.wait()
    f0, f1 = field[0], field[1]
    before = jnp.where(sl > 0, halo[0, 0:LB, :], 0.0)
    after = jnp.where(sl < ns - 1, halo[1, 0:LB, :], 0.0)
    first = jnp.concatenate([f0[LB:], after], axis=0) - jnp.concatenate([before, f0[:edge]], axis=0)
    below = jnp.where(me > 0, halo[2], 0.0)
    above = jnp.where(me < nb - 1, halo[3], 0.0)
    inner = lax.rem(rows16, LB)
    plus = jnp.where(inner == LB - 1, pltpu.roll(above, LB - 1, 0), pltpu.roll(f1, buckets - 1, 0))
    minus = jnp.where(inner == 0, pltpu.roll(below, buckets - (LB - 1), 0), pltpu.roll(f1, 1, 0))
    result = 0.5 * first + 0.5 * (plus - minus)
    out[2] = result + 0.5 * third

    wait_sent(ask, 0)
    wait_sent(pay, 1)
    for sweep in range(ITERS):
        wait_sent(wsend.at[sweep], 2 + 2 * sweep)
        wait_sent(vsend.at[sweep], 3 + 2 * sweep)


def solution(mesh):
    nb, ns = mesh.shape["bricks"], mesh.shape["slab"]

    def on_device(
        part_pos, part_mass, cell_pos, cell_mass, cell_scale,
        req_tile, tile_bucket, tile_slot, tile_count, lagr_index,
    ):
        buckets, tiles = part_pos.shape[2] // TS, cell_pos.shape[2] // TS
        count = tile_bucket.shape[1]
        vmem = pl.BlockSpec(memory_space=pltpu.VMEM)
        smem = pl.BlockSpec(memory_space=pltpu.SMEM)
        away = pl.BlockSpec(memory_space=pl.ANY)
        out = pl.pallas_call(
            functools.partial(kernel, nb, ns, buckets, tiles, count),
            out_shape=jax.ShapeDtypeStruct((3, buckets, TS), F32),
            in_specs=[away] * 8 + [smem, away],
            out_specs=vmem,
            scratch_shapes=[
                pltpu.VMEM((3, 1, buckets * TS), F32),
                pltpu.VMEM((1, buckets * TS), F32),
                pltpu.VMEM((3, 1, tiles * TS), F32),
                pltpu.VMEM((1, tiles * TS), F32),
                pltpu.VMEM((1, tiles * TS), F32),
                pltpu.VMEM((1, nb), I32),
                pltpu.VMEM((1, count), I32),
                pltpu.VMEM((1, count), I32),
                pltpu.VMEM((1, buckets * TS), I32),
                pltpu.SemaphoreType.DMA((9,)),
                pltpu.VMEM((nb, TS), I32),
                pltpu.VMEM((nb, TS), I32),
                pltpu.VMEM((8, TL), I32),
                pltpu.SMEM((8, TL), I32),
                pltpu.VMEM((3, buckets, TS), F32),
                pltpu.VMEM((3, tiles, TS), F32),
                pltpu.VMEM((3, tiles, TS), F32),
                pltpu.VMEM((3, buckets, TS, TS), F32),
                pltpu.VMEM((buckets, TS, TS), F32),
                pltpu.VMEM((buckets, TS, TS), F32),
                pltpu.VMEM((count, TS, TS), F32),
                pltpu.VMEM((count, TS, TS), F32),
                pltpu.VMEM((count, 8, TS), F32),
                pltpu.VMEM((3 * tiles, 4 * TS), BF16),
                pltpu.VMEM((nb, 4, TS), F32),
                pltpu.VMEM((nb, 4, TS), F32),
                pltpu.VMEM((ITERS, nb, TS), F32),
                pltpu.VMEM((ITERS, nb, TS), F32),
                pltpu.VMEM((ITERS, nb, TS), F32),
                pltpu.VMEM((ITERS, nb, TS), F32),
                pltpu.VMEM((nb, 8, TS), F32),
                pltpu.VMEM((count, 2 * TS, TS), BF16),
                pltpu.VMEM((4, buckets, TS), F32),
                pltpu.VMEM((buckets * TS, TS), BF16),
                pltpu.VMEM((2, buckets, TS), F32),
                pltpu.VMEM((4, buckets, TS), F32),
                pltpu.SemaphoreType.DMA((2 + 2 * ITERS,)),
                pltpu.SemaphoreType.DMA((2 + 2 * ITERS,)),
                pltpu.SemaphoreType.DMA((2, 4)),
                pltpu.SemaphoreType.DMA,
            ],
            name="sinkhorn",
            compiler_params=pltpu.CompilerParams(
                collective_id=0, has_side_effects=True, vmem_limit_bytes=56 << 20
            ),
        )(
            part_pos.transpose(1, 0, 2), part_mass, cell_pos.transpose(1, 0, 2), cell_mass, cell_scale,
            req_tile.T, tile_bucket, tile_slot, tile_count, lagr_index,
        )
        return out[0].reshape(1, -1), out[1].reshape(1, -1), out[2].reshape(-1, LB, TS)

    device = P(("bricks", "slab"))
    return jax.shard_map(
        on_device,
        mesh=mesh,
        in_specs=(device,) * 10,
        out_specs=(device, device, P("slab", "bricks", None)),
        check_vma=False,
    )
```

```python
import functools
import math

import jax
import jax.numpy as jnp
from jax import lax
from jax.experimental import pallas as pl
from jax.experimental.pallas import tpu as pltpu
from jax.sharding import PartitionSpec as P

TS = 128
EPS = 0.05
ITERS = 2
LB = 4
SCALE = math.sqrt(2.0 / (EPS * math.log(2.0)))
CENTER = (0.125, 0.125, 0.5)
HALF_LN2 = 0.5 * math.log(2.0)
MESH = pl.DeviceIdType.MESH
F32, BF16, I32 = jnp.float32, jnp.bfloat16, jnp.int32
TL = 256


def split3(a):
    hi = a.astype(BF16)
    rest = a - hi.astype(F32)
    mid = rest.astype(BF16)
    return hi, mid, (rest - mid.astype(F32)).astype(BF16)


def pick(hot, rows):
    hi, mid, lo = split3(rows)
    return jnp.dot(
        jnp.concatenate([hot, hot, hot], axis=1),
        jnp.concatenate([hi, mid, lo], axis=0),
        preferred_element_type=F32,
    )


def iota(shape, axis):
    return lax.broadcasted_iota(I32, shape, axis)


def kernel(
    nb, ns, buckets, tiles, count,
    pos_far, mass_far, cpos_far, cmass_far, cscale_far, req_far, tb_far, ts_far, cnt_in, lagr_far,
    out,
    pos_in, mass_in, cpos_in, cmass_in, cscale_in, req_in, tb_in, ts_in, lagr_in, isem,
    ask, asked, lists_v, lists, xs, ys, rowsets, xb, mb, ub, kt, seg, colseg,
    offer, pay, cells, wsend, wrecv, vsend, vrecv, basis, turned, sums, hot_l, field, halo,
    ssem, rsem, hsem, lsem,
):
    me, sl = lax.axis_index("bricks"), lax.axis_index("slab")
    up, down = lax.rem(me + 1, nb), lax.rem(me + nb - 1, nb)
    right, left = lax.rem(sl + 1, ns), lax.rem(sl + ns - 1, ns)

    core, z, y = lax.rem(me, 2), lax.rem(me // 2, 8), me // 16

    def peer_at(k):
        turn_z, turn_y = k // 8, lax.rem(k // 2, 4)
        step_z = 4 + (turn_z + 1) // 2 * (1 - 2 * lax.rem(turn_z, 2))
        step_y = 2 + (turn_y + 1) // 2 * (1 - 2 * lax.rem(turn_y, 2))
        return lax.rem(y + step_y, 4) * 16 + lax.rem(z + step_z, 8) * 2 + lax.rem(core + k + 1, 2)

    def place_of(slot):
        def turn(step):
            return jnp.where(step < 0, -2 * step - 1, 2 * step)

        off_y = (((slot >> 4) + (4 - y)) & 3) - 2
        off_z = ((((slot >> 1) & 7) + (8 - z)) & 7) - 4
        off_core = ((slot & 1) + (2 - core)) & 1
        return turn(off_z) * 8 + turn(off_y) * 2 + 1 - off_core

    barrier = pltpu.get_barrier_semaphore()

    def greet(k, carry):
        pl.semaphore_signal(barrier, inc=1, device_id=(peer_at(k), sl), device_id_type=MESH)
        return carry

    lax.fori_loop(0, nb - 1, greet, 0, unroll=7)
    for other in (left, right):
        pl.semaphore_signal(barrier, inc=1, device_id=(me, other), device_id_type=MESH)

    loads = [
        pltpu.make_async_copy(far, near, isem.at[i])
        for i, (far, near) in enumerate(
            (
                (req_far, req_in), (tb_far, tb_in), (ts_far, ts_in), (pos_far, pos_in),
                (mass_far, mass_in), (cpos_far, cpos_in), (cmass_far, cmass_in),
                (cscale_far, cscale_in), (lagr_far, lagr_in),
            )
        )
    ]
    for load in loads:
        load.start()

    def send_all(src, dst, phase):
        def one(k, carry):
            peer = peer_at(k)
            pltpu.make_async_remote_copy(
                src_ref=src.at[peer], dst_ref=dst.at[me],
                send_sem=ssem.at[phase], recv_sem=rsem.at[phase],
                device_id=(peer, sl), device_id_type=MESH,
            ).start()
            return carry

        lax.fori_loop(0, nb - 1, one, 0, unroll=7)
        pltpu.make_async_copy(src.at[me], dst.at[me], rsem.at[phase]).start()

    def wait_all(dst, phase):
        pltpu.make_async_copy(dst, dst, rsem.at[phase]).wait()

    def wait_sent(src, phase):
        part = src.at[pl.ds(0, nb - 1)]
        pltpu.make_async_copy(part, part, ssem.at[phase]).wait()

    for load in loads:
        load.wait()
    ask[...] = jnp.broadcast_to(req_in[...], (TS, nb)).T

    lane = iota((1, TL), 1)
    live = lane < cnt_in[0]
    tb = jnp.concatenate([tb_in[...], jnp.zeros((1, TL - count), I32)], axis=1)
    ts = jnp.concatenate([ts_in[...], jnp.zeros((1, TL - count), I32)], axis=1)
    key_b = jnp.where(live, tb, buckets)
    key_s = jnp.where(live, place_of(ts), nb)
    uni_b, uni_s = key_b * TL + lane, key_s * TL + lane
    zero = jnp.zeros((1, TL), I32)
    cols = jnp.concatenate([uni_b, uni_s, tb, ts, key_b, key_s, zero, zero], axis=0).T
    col_tb, col_ts, col_kb, col_ks = (cols[:, i : i + 1] for i in range(2, 6))

    def total(where, value):
        return jnp.sum(jnp.where(where, value, 0), axis=0, keepdims=True)

    rank_b = total(cols[:, 0:1] < uni_b, 1)
    rank_s = total(cols[:, 1:2] < uni_s, 1)
    ranks = jnp.concatenate([rank_b, rank_s] + [zero] * 6, axis=0).T
    wide = iota((TL, TL), 1)
    at_b, at_s = ranks[:, 0:1] == wide, ranks[:, 1:2] == wide

    def same(row):
        return jnp.where((row == pltpu.roll(row, 1, 1)) & (lane > 0), 1, 0)

    def within(row, most):
        return jnp.minimum(jnp.maximum(row, 0), most)

    lists_v[0:1, :] = within(total(at_b, col_tb), buckets - 1)
    lists_v[1:2, :] = within(total(at_b, col_ts), nb - 1)
    lists_v[2:3, :] = same(total(at_b, col_kb))
    lists_v[3:4, :] = within(total(at_s, ranks[:, 0:1]), count - 1)
    lists_v[4:5, :] = within(total(at_s, col_tb), buckets - 1)
    lists_v[5:6, :] = same(total(at_s, col_ks))
    lists_v[6:7, :] = within(total(col_kb <= wide, 1) - 1, count - 1)
    lists_v[7:8, :] = within(total(col_ks <= wide, 1) - 1, count - 1)
    to_smem = pltpu.make_async_copy(lists_v, lists, lsem)
    to_smem.start()

    for q in range(buckets):
        part = pl.ds(q * TS, TS)
        rowsets[0, q : q + 1, :] = mass_in[:, part]
        for m in range(3):
            xs[m, q : q + 1, :] = (pos_in[m, :, part] - CENTER[m]) * SCALE
    for q in range(tiles):
        part = pl.ds(q * TS, TS)
        rowsets[1, q : q + 1, :] = cmass_in[:, part]
        rowsets[2, q : q + 1, :] = cscale_in[:, part]
        for m in range(3):
            ys[m, q : q + 1, :] = (cpos_in[m, :, part] - CENTER[m]) * SCALE
    ysq = ys[0] * ys[0] + ys[1] * ys[1] + ys[2] * ys[2]
    scaled = rowsets[2] * jnp.exp2(-0.5 * ysq)
    offer[...] = jnp.concatenate(split3(jnp.concatenate([ys[0], ys[1], ys[2], scaled], axis=1)), axis=0)

    pl.semaphore_wait(barrier, nb + 1)
    send_all(ask, asked, 0)

    columns = jnp.concatenate([xs[0], xs[1], xs[2], rowsets[0]], axis=0).T
    for q in range(buckets):
        for m in range(3):
            xb[m, q] = jnp.broadcast_to(columns[:, m * buckets + q : m * buckets + q + 1], (TS, TS))
        mb[q] = jnp.broadcast_to(columns[:, 3 * buckets + q : 3 * buckets + q + 1], (TS, TS))

    spots = jnp.concatenate(
        [lagr_in[:, pl.ds(q * TS, TS)] for q in range(buckets)] + [jnp.zeros((TS - buckets, TS), I32)], axis=0
    )
    spots_c = (spots & (TS - 1)).T
    for q in range(buckets):
        hot_l[pl.ds(q * TS, TS), :] = jnp.where(
            spots_c[:, q : q + 1] == iota((TS, TS), 1), 1.0, 0.0
        ).astype(BF16)

    wait_all(asked, 0)
    asks = asked[...].astype(F32)
    hot = jnp.where(asks[:, 0:tiles] == iota((nb, tiles), 1).astype(F32), 1.0, 0.0).astype(BF16)
    chosen = jnp.dot(jnp.concatenate([hot, hot, hot], axis=1), offer[...], preferred_element_type=F32)
    for m in range(4):
        pay[:, m, :] = chosen[:, m * TS : (m + 1) * TS]
    send_all(pay, cells, 1)
    cmass_of = pick(hot, rowsets[1])
    asks_t = asks.T
    twins = jnp.where(asks[:, 0:nb] == asks_t[0:nb, :], 1.0, 0.0).astype(BF16)
    hot_t = jnp.where(asks_t[0:tiles, :] == iota((tiles, nb), 0).astype(F32), 1.0, 0.0).astype(BF16)

    to_smem.wait()
    wait_all(cells, 1)

    def build(k, total):
        b, s = lists[0, k], lists[1, k]
        exponent = xb[0, b] * cells[s, 0:1] + xb[1, b] * cells[s, 1:2] + xb[2, b] * cells[s, 2:3]
        tile = jnp.exp2(exponent)
        kt[k] = tile
        total = jnp.where(lists[2, k] > 0, total, 0.0) + tile * cells[s, 3:4]
        seg[k] = total
        return total

    lax.fori_loop(0, count, build, jnp.zeros((TS, TS), F32), unroll=8)

    def row_pass(value):
        def step(k, total):
            total = jnp.where(lists[2, k] > 0, total, 0.0) + kt[k] * value(lists[1, k])
            seg[k] = total
            return total

        lax.fori_loop(0, count, step, jnp.zeros((TS, TS), F32), unroll=8)

    def col_pass(sweep):
        def scale(q, carry):
            ub[q] = mb[q] / jnp.sum(seg[lists[6, q]], axis=1, keepdims=True)
            return carry

        lax.fori_loop(0, buckets, scale, 0, unroll=8)

        def step(k, total):
            product = kt[lists[3, k]] * ub[lists[4, k]]
            part = jnp.sum(product.reshape(TS // 8, 8, TS), axis=0)
            total = jnp.where(lists[5, k] > 0, total, 0.0) + part
            colseg[k] = total
            return total

        group = 16

        def steps_and_sends(block, total, sends):
            first = block * group
            for i in range(group):
                total = step(count - nb + first + i, total)
            for i in range(group):
                wsend[sweep, pl.ds(first + i, 1), :] = jnp.sum(
                    colseg[lists[7, first + i]], axis=0, keepdims=True
                )
            for i in range(sends):
                pltpu.make_async_remote_copy(
                    src_ref=wsend.at[sweep, first + i], dst_ref=wrecv.at[sweep, me],
                    send_sem=ssem.at[2 + 2 * sweep], recv_sem=rsem.at[2 + 2 * sweep],
                    device_id=(peer_at(first + i), sl), device_id_type=MESH,
                ).start()
            return total

        total = lax.fori_loop(0, count - nb, step, jnp.zeros((8, TS), F32), unroll=8)
        total = lax.fori_loop(
            0, nb // group - 1, lambda block, carry: steps_and_sends(block, carry, group), total
        )
        steps_and_sends(nb // group - 1, total, group - 1)
        pltpu.make_async_copy(
            wsend.at[sweep, nb - 1], wrecv.at[sweep, me], rsem.at[2 + 2 * sweep]
        ).start()

    def turn(quarter):
        def step(k, carry):
            flat = kt[k].T
            hi = flat.astype(BF16)
            turned[k, 0:TS, :] = hi
            turned[k, TS : 2 * TS, :] = (flat - hi.astype(F32)).astype(BF16)
            return carry

        lax.fori_loop(quarter * count // 4, (quarter + 1) * count // 4, step, 0, unroll=2)

    for sweep in range(ITERS):
        if sweep:
            row_pass(lambda s: vrecv[0, pl.ds(s, 1), :])
        col_pass(sweep)
        turn(2 * sweep)
        wait_all(wrecv.at[sweep], 2 + 2 * sweep)
        vsend[sweep] = cmass_of / pick(twins, wrecv[sweep])
        send_all(vsend.at[sweep], vrecv.at[sweep], 3 + 2 * sweep)
        turn(2 * sweep + 1)
        if sweep == 0:
            for half in range(2):
                for m in range(3):
                    basis[:, 4 * half + m, :] = cells[:, m, :]
                basis[:, 4 * half + 3, :] = jnp.ones((nb, TS), F32)
        if sweep == ITERS - 1:
            cell_v = rowsets[1] / pick(hot_t, wrecv[sweep])
            potential = jnp.log(cell_v) + HALF_LN2 * ysq
            out[1] = potential
        wait_all(vrecv.at[sweep], 3 + 2 * sweep)

    upper = iota((8, TS), 0) < 4

    def last_step(k, total):
        s = lists[1, k]
        value = basis[s] * vrecv[ITERS - 1, pl.ds(s, 1), :]
        hi = value.astype(BF16).astype(F32)
        left_side = jnp.where(upper, hi, value - hi).astype(BF16)
        part = jnp.dot(
            jnp.concatenate([left_side, left_side], axis=1), turned[k], preferred_element_type=F32
        )
        total = jnp.where(lists[2, k] > 0, total, 0.0) + part
        colseg[k] = total
        return total

    lax.fori_loop(0, count, last_step, jnp.zeros((8, TS), F32), unroll=36)
    for q in range(buckets):
        both = colseg[lists[6, q]]
        both = both[0:4, :] + both[4:8, :]
        for m in range(4):
            sums[m, q : q + 1, :] = both[m : m + 1, :]
    s0 = sums[3]

    spot_row = lagr_in[...] // TS
    rows16 = iota((buckets, TS), 0)
    masks = [spot_row[:, q * TS : (q + 1) * TS] == rows16 for q in range(buckets)]

    def placed(axes):
        stack = []
        for m in axes:
            shift = (sums[m] / s0 - xs[m]) * (1.0 / SCALE)
            hi = shift.astype(BF16).astype(F32)
            for part in (hi, shift - hi):
                stack.append(
                    jnp.concatenate(
                        [
                            jnp.where(masks[q], part[q : q + 1, :], 0.0).astype(BF16)
                            for q in range(buckets)
                        ],
                        axis=1,
                    )
                )
        both = jnp.dot(jnp.concatenate(stack, axis=0), hot_l[...], preferred_element_type=F32)
        return [
            both[2 * i * buckets : (2 * i + 1) * buckets, :]
            + both[(2 * i + 1) * buckets : (2 * i + 2) * buckets, :]
            for i in range(len(axes))
        ]

    field[0], field[1] = placed((0, 1))
    edge = buckets - LB
    sends = [
        (field.at[0, pl.ds(edge, LB)], halo.at[0, pl.ds(0, LB)], (me, right)),
        (field.at[0, pl.ds(0, LB)], halo.at[1, pl.ds(0, LB)], (me, left)),
        (field.at[1], halo.at[2], (up, sl)),
        (field.at[1], halo.at[3], (down, sl)),
    ]
    copies = [
        pltpu.make_async_remote_copy(
            src_ref=src, dst_ref=dst, send_sem=hsem.at[0, i], recv_sem=hsem.at[1, i],
            device_id=device, device_id_type=MESH,
        )
        for i, (src, dst, device) in enumerate(sends)
    ]
    for copy in copies:
        copy.start()
    xsq = xs[0] * xs[0] + xs[1] * xs[1] + xs[2] * xs[2]
    potential = jnp.log(rowsets[0] / s0) + HALF_LN2 * xsq
    out[0] = potential
    (f2,) = placed((2,))
    lanes = iota((buckets, TS), 1)
    third = jnp.where(lanes == TS - 1, 0.0, pltpu.roll(f2, TS - 1, 1)) - jnp.where(
        lanes == 0, 0.0, pltpu.roll(f2, 1, 1)
    )
    for copy in copies:
        copy.wait()
    f0, f1 = field[0], field[1]
    before = jnp.where(sl > 0, halo[0, 0:LB, :], 0.0)
    after = jnp.where(sl < ns - 1, halo[1, 0:LB, :], 0.0)
    first = jnp.concatenate([f0[LB:], after], axis=0) - jnp.concatenate([before, f0[:edge]], axis=0)
    below = jnp.where(me > 0, halo[2], 0.0)
    above = jnp.where(me < nb - 1, halo[3], 0.0)
    inner = lax.rem(rows16, LB)
    plus = jnp.where(inner == LB - 1, pltpu.roll(above, LB - 1, 0), pltpu.roll(f1, buckets - 1, 0))
    minus = jnp.where(inner == 0, pltpu.roll(below, buckets - (LB - 1), 0), pltpu.roll(f1, 1, 0))
    result = 0.5 * first + 0.5 * (plus - minus)
    out[2] = result + 0.5 * third

    wait_sent(ask, 0)
    wait_sent(pay, 1)
    for sweep in range(ITERS):
        wait_sent(wsend.at[sweep], 2 + 2 * sweep)
        wait_sent(vsend.at[sweep], 3 + 2 * sweep)


def solution(mesh):
    nb, ns = mesh.shape["bricks"], mesh.shape["slab"]

    def on_device(
        part_pos, part_mass, cell_pos, cell_mass, cell_scale,
        req_tile, tile_bucket, tile_slot, tile_count, lagr_index,
    ):
        buckets, tiles = part_pos.shape[2] // TS, cell_pos.shape[2] // TS
        count = tile_bucket.shape[1]
        vmem = pl.BlockSpec(memory_space=pltpu.VMEM)
        smem = pl.BlockSpec(memory_space=pltpu.SMEM)
        away = pl.BlockSpec(memory_space=pl.ANY)
        out = pl.pallas_call(
            functools.partial(kernel, nb, ns, buckets, tiles, count),
            out_shape=jax.ShapeDtypeStruct((3, buckets, TS), F32),
            in_specs=[away] * 8 + [smem, away],
            out_specs=vmem,
            scratch_shapes=[
                pltpu.VMEM((3, 1, buckets * TS), F32),
                pltpu.VMEM((1, buckets * TS), F32),
                pltpu.VMEM((3, 1, tiles * TS), F32),
                pltpu.VMEM((1, tiles * TS), F32),
                pltpu.VMEM((1, tiles * TS), F32),
                pltpu.VMEM((1, nb), I32),
                pltpu.VMEM((1, count), I32),
                pltpu.VMEM((1, count), I32),
                pltpu.VMEM((1, buckets * TS), I32),
                pltpu.SemaphoreType.DMA((9,)),
                pltpu.VMEM((nb, TS), I32),
                pltpu.VMEM((nb, TS), I32),
                pltpu.VMEM((8, TL), I32),
                pltpu.SMEM((8, TL), I32),
                pltpu.VMEM((3, buckets, TS), F32),
                pltpu.VMEM((3, tiles, TS), F32),
                pltpu.VMEM((3, tiles, TS), F32),
                pltpu.VMEM((3, buckets, TS, TS), F32),
                pltpu.VMEM((buckets, TS, TS), F32),
                pltpu.VMEM((buckets, TS, TS), F32),
                pltpu.VMEM((count, TS, TS), F32),
                pltpu.VMEM((count, TS, TS), F32),
                pltpu.VMEM((count, 8, TS), F32),
                pltpu.VMEM((3 * tiles, 4 * TS), BF16),
                pltpu.VMEM((nb, 4, TS), F32),
                pltpu.VMEM((nb, 4, TS), F32),
                pltpu.VMEM((ITERS, nb, TS), F32),
                pltpu.VMEM((ITERS, nb, TS), F32),
                pltpu.VMEM((ITERS, nb, TS), F32),
                pltpu.VMEM((ITERS, nb, TS), F32),
                pltpu.VMEM((nb, 8, TS), F32),
                pltpu.VMEM((count, 2 * TS, TS), BF16),
                pltpu.VMEM((4, buckets, TS), F32),
                pltpu.VMEM((buckets * TS, TS), BF16),
                pltpu.VMEM((2, buckets, TS), F32),
                pltpu.VMEM((4, buckets, TS), F32),
                pltpu.SemaphoreType.DMA((2 + 2 * ITERS,)),
                pltpu.SemaphoreType.DMA((2 + 2 * ITERS,)),
                pltpu.SemaphoreType.DMA((2, 4)),
                pltpu.SemaphoreType.DMA,
            ],
            name="sinkhorn",
            compiler_params=pltpu.CompilerParams(
                collective_id=0, has_side_effects=True, vmem_limit_bytes=56 << 20
            ),
        )(
            part_pos.transpose(1, 0, 2), part_mass, cell_pos.transpose(1, 0, 2), cell_mass, cell_scale,
            req_tile.T, tile_bucket, tile_slot, tile_count, lagr_index,
        )
        return out[0].reshape(1, -1), out[1].reshape(1, -1), out[2].reshape(-1, LB, TS)

    device = P(("bricks", "slab"))
    return jax.shard_map(
        on_device,
        mesh=mesh,
        in_specs=(device,) * 10,
        out_specs=(device, device, P("slab", "bricks", None)),
        check_vma=False,
    )
```
